512 devices in a mesh: dp: 32 (over y, z_lo), tp: 16 (over z_hi, x, core).
Axes of the slice: x: 4, y: 4, z: 16 (z_hi: 2, z_lo: 8; z = z_hi * 8 + z_lo), core: 2. Of those that a mesh axis runs over, the one named last changes fastest.
Arguments:
- patches: bfloat16 [64, 576, 1024], P('dp', 'tp'), may hold values from -6 to 6
- image_slot: int32 [64], P('dp'), may hold values from 0 to 1, as said below
- trainer_blocks: int32 [16], replicated, may hold values from 0 to 15, each once
- conv_weight: bfloat16 [9216, 1024], P('dp', 'tp'), may hold values from -0.0625 to 0.0625
- proj_weight: bfloat16 [1024, 8192], P('dp', 'tp'), may hold values from -0.1875 to 0.1875
Outputs:
- vision_tokens: bfloat16 [64, 144, 8192], P('dp', None, 'tp')
The draws below stay inside these ranges and needn't reach their ends.
Inputs may be any that keep to these rules, and one draw needn't show every extreme that they name: `image_slot`: each aligned block of 2 entries, one block for each index of dp, is a permutation of 0 to 1. `trainer_blocks`: a permutation.
All inputs are finite; a program needn't handle non-finite values.
Results may differ from the reference program's by a relative error of at most 0.005.
Values may be sent and summed in bfloat16 or wider, within the bound.
A program may use at most 64 MiB of HBM per device.

```python
import jax
import jax.numpy as jnp
from jax import lax

C = 1024
LLM = 8192
GRID = 24
IMG_DP = 2
POOL = 12
IMAGES = 64
BLOCKS = 16


def draw_image_slot(key, part):
    key = jax.random.fold_in(key, 11)
    keys = jax.random.split(key, IMAGES // IMG_DP)
    orders = jax.vmap(lambda single_key: jax.random.permutation(single_key, IMG_DP))(keys)
    return orders.reshape(IMAGES).astype(jnp.int32)


def steps_of(own_key, extent, cuts, least, largest):
    loudness = 1.0
    for position, shards_of in cuts:
        steps = jax.random.uniform(jax.random.fold_in(jax.random.fold_in(own_key, 6), position), (shards_of,), jnp.float32, least / len(cuts), largest / len(cuts))
        loudness = loudness * jnp.repeat(jnp.exp(steps), extent[position] // shards_of).reshape((-1,) + (1,) * (len(extent) - 1 - position))
    return loudness


def noise(stream_key, extent, deviation, bound, cuts=(), kind=jnp.bfloat16):
    result = deviation * jax.random.normal(stream_key, extent, jnp.float32)
    if cuts:
        result = result * steps_of(stream_key, extent, cuts, -0.22, 0.18)
    return jnp.clip(result, -bound, bound).astype(kind)


def setup_inputs(seed: int = 0) -> dict:
    key_list = jax.random.split(jax.random.key(seed), 6)
    return {
        "patches": noise(key_list[0], (IMAGES, GRID * GRID, C), 1.0, 6.0, ((0, 32), (1, 16))),
        "image_slot": draw_image_slot(jax.random.fold_in(key_list[5], 71), 0),
        "trainer_blocks": jax.random.permutation(key_list[2], BLOCKS).astype(jnp.int32),
        "conv_weight": noise(key_list[3], (9 * C, C), (9 * C) ** -0.5, 0.0625, ((0, 32), (1, 16))),
        "proj_weight": noise(key_list[4], (C, LLM), C ** -0.5, 0.1875, ((0, 32), (1, 16))),
    }


def reference(patches, image_slot, trainer_blocks, conv_weight, proj_weight):
    block_count = trainer_blocks.shape[0]
    holder = jnp.argsort(trainer_blocks).astype(jnp.int32)
    conv_logical = conv_weight.reshape(9 * C, block_count, C // block_count)[:, holder].reshape(9 * C, C)
    proj_logical = proj_weight.reshape(C, block_count, LLM // block_count)[:, holder].reshape(C, LLM)
    base_index = (jnp.arange(IMAGES, dtype=jnp.int32) // IMG_DP) * IMG_DP
    source = (base_index + image_slot).astype(jnp.int32)

    def single(index):
        image = lax.dynamic_index_in_dim(patches, index, 0, keepdims=False).reshape(GRID, GRID, C)
        padded = jnp.pad(image, ((1, 1), (1, 1), (0, 0)))
        total = jnp.zeros((GRID * GRID, C), jnp.float32)
        for tap in range(9):
            row_shift = tap // 3
            col_shift = tap % 3
            window = padded[row_shift:row_shift + GRID, col_shift:col_shift + GRID, :].reshape(GRID * GRID, C)
            total = total + jnp.dot(window, conv_logical[tap * C:(tap + 1) * C], preferred_element_type=jnp.float32)
        feature = image.reshape(GRID * GRID, C).astype(jnp.float32) + jax.nn.silu(total)
        pooled = feature.reshape(POOL, 2, POOL, 2, C).mean(axis=(1, 3)).reshape(POOL * POOL, C).astype(jnp.bfloat16)
        return jnp.dot(pooled, proj_logical, preferred_element_type=jnp.float32).astype(jnp.bfloat16)

    return lax.map(single, source)
```

```python
import functools

import jax
import jax.numpy as jnp
from jax import lax
from jax.experimental import pallas as pl
from jax.experimental.pallas import tpu as pltpu
from jax.sharding import PartitionSpec as P

MESH = pl.DeviceIdType.MESH

GRID = 24
NX, NY, NZ = 4, 4, 8
SLOTS = 2 * NX
SLOT_ROWS = 80
CHIP_ROWS = 72


class Place:
    def __init__(self):
        d = lax.axis_index("dp")
        t = lax.axis_index("tp")
        self.y, self.z = d // NZ, lax.rem(d, NZ)
        self.h, self.x, self.c = t // (2 * NX), lax.rem(t // 2, NX), lax.rem(t, 2)
        self.d, self.t = d, t
        self.slot = self.h * NX + self.x

    def at(self, y=None, z=None, h=None, x=None, c=None):
        y = self.y if y is None else y
        z = self.z if z is None else z
        h = self.h if h is None else h
        x = self.x if x is None else x
        c = self.c if c is None else c
        return (y * NZ + z, h * (2 * NX) + x * 2 + c)

    def sibling(self):
        return self.at(c=1 - self.c)

    def flip(self):
        return self.at(h=1 - self.h)


def plus(value, step, size):
    return lax.rem(value + step, size)


def kernel(
    tb_ref,
    slot_ref,
    patches,
    conv,
    proj,
    out_ref,
    tokens,
    halves,
    grid_img,
    weights,
    z_ref,
    fs_ref,
    pooled,
    proj_all,
    proj_cols,
    proj_perm,
    loc,
    ce_s,
    ce_r,
    wz_s,
    wz_r,
    wy_s,
    wy_r,
    wd_s,
    wd_r,
    gz_s,
    gz_r,
    gx_s,
    gx_r,
    pz_s,
    pz_r,
    px_s,
    px_r,
    pd_s,
    pd_r,
    qz_s,
    qz_r,
    qy_s,
    qy_r,
    oz_s,
    oz_r,
    ox_s,
    ox_r,
    od_s,
    od_r,
):
    me = Place()
    c, h, x, y, z, d = me.c, me.h, me.x, me.y, me.z, me.d
    other = 1 - c
    sibling, flip = me.sibling(), me.flip()
    my_slot = me.slot
    flip_slot = (1 - h) * NX + x

    def remote(src, dst, send, recv, where):
        return pltpu.make_async_remote_copy(
            src_ref=src, dst_ref=dst, send_sem=send, recv_sem=recv, device_id=where, device_id_type=MESH
        )

    def await_recv(dst, recv):
        remote(dst, dst, recv, recv, sibling).wait_recv()

    def await_send(src, send):
        remote(src, src, send, send, sibling).wait_send()

    barrier = pltpu.get_barrier_semaphore()

    def greet(where):
        pl.semaphore_signal(barrier, inc=1, device_id=where, device_id_type=MESH)

    greet(flip)
    for k in range(1, NZ):
        greet(me.at(z=plus(z, k, NZ)))
    for k in range(1, NX):
        greet(me.at(x=plus(x, k, NX)))
    for k in range(1, NY):
        greet(me.at(y=plus(y, k, NY)))
    greet(sibling)

    own_rows = pl.ds(pl.multiple_of(c * 144, 16), 144)
    other_rows = pl.ds(pl.multiple_of(other * 144, 16), 144)
    local = [
        pltpu.make_async_copy(patches.at[c], tokens.at[c], loc.at[0]),
        pltpu.make_async_copy(conv.at[own_rows], halves.at[c], loc.at[1]),
        pltpu.make_async_copy(proj, proj_all.at[c, my_slot], loc.at[2]),
    ]
    for copy in local:
        copy.start()

    row = lax.broadcasted_iota(jnp.int32, (1024, 128), 0)
    lane = lax.broadcasted_iota(jnp.int32, (1024, 128), 1)
    first = tb_ref[2 * my_slot] * 64
    second = tb_ref[2 * my_slot + 1] * 64 - 64
    wanted = lane + jnp.where(lane < 64, first, second)
    weights[pl.ds(9 * 1024, 1024), :] = jnp.where(row == wanted, 1.0, 0.0).astype(jnp.bfloat16)

    for copy in local:
        copy.wait()
    pl.semaphore_wait(barrier, 1 + (NZ - 1) + (NX - 1) + (NY - 1) + 1)

    ce_conv = remote(conv.at[other_rows], halves.at[c], ce_s.at[0], ce_r.at[0], sibling)
    ce_conv.start()
    ce_img = remote(patches.at[other], tokens.at[c], ce_s.at[1], ce_r.at[1], sibling)
    ce_img.start()
    own_proj = proj_all.at[c, my_slot]
    remote(own_proj, own_proj, pz_s, pz_r, flip).start()
    for k in range(1, NX):
        remote(own_proj, own_proj, px_s.at[k - 1], px_r.at[k - 1], me.at(x=plus(x, k, NX))).start()

    def shard(dp, core):
        return weights.at[pl.ds(pl.multiple_of(dp * 288 + core * 144, 16), 144)]

    await_recv(halves.at[other], ce_r.at[0])
    own_shard = shard(d, c)
    own_shard[...] = jnp.concatenate([halves[0], halves[1]], axis=1)
    for k in range(1, NZ):
        remote(own_shard, own_shard, wz_s.at[k - 1], wz_r.at[k - 1], me.at(z=plus(z, k, NZ))).start()

    await_recv(tokens.at[other], ce_r.at[1])
    chip_tokens = jnp.concatenate(
        [tokens[0].astype(jnp.float32), tokens[1].astype(jnp.float32), jnp.zeros((SLOT_ROWS - CHIP_ROWS, 1024), jnp.float32)],
        axis=0,
    )

    def image(slot):
        return grid_img.at[pl.ds(pl.multiple_of(slot * SLOT_ROWS, 16), SLOT_ROWS)]

    own_img = image(my_slot)
    own_img[...] = chip_tokens.astype(jnp.bfloat16)
    remote(own_img, own_img, gz_s, gz_r, flip).start()
    for k in range(1, NX):
        remote(own_img, own_img, gx_s.at[k - 1], gx_r.at[k - 1], me.at(x=plus(x, k, NX))).start()

    def shard_to_y(k):
        piece = shard(y * NZ + lax.rem(z - k + NZ, NZ), c)
        for j in range(1, NY):
            remote(
                piece, piece, wy_s.at[(j - 1) * NZ + k], wy_r.at[(j - 1) * NZ + k], me.at(y=plus(y, j, NY))
            ).start()

    shard_to_y(0)

    @pl.loop(1, NZ)
    def _(k):
        await_recv(shard(y * NZ + lax.rem(z - k + NZ, NZ), c), wz_r.at[k - 1])
        shard_to_y(k)

    def to_sibling(dp, index):
        piece = shard(dp, c)
        remote(piece, piece, wd_s.at[index], wd_r.at[index], sibling).start()

    @pl.loop(0, NZ)
    def _(k):
        to_sibling(y * NZ + lax.rem(z - k + NZ, NZ), k)

    flip_proj = proj_all.at[c, flip_slot]
    await_recv(flip_proj, pz_r)
    for k in range(1, NX):
        remote(flip_proj, flip_proj, px_s.at[2 + k], px_r.at[2 + k], me.at(x=plus(x, k, NX))).start()

    flip_img = image(flip_slot)
    await_recv(flip_img, gz_r)
    for k in range(1, NX):
        remote(flip_img, flip_img, gx_s.at[2 + k], gx_r.at[2 + k], me.at(x=plus(x, k, NX))).start()

    for k in range(1, NX):
        src_x = plus(x, NX - k, NX)
        await_recv(proj_all.at[c, h * NX + src_x], px_r.at[k - 1])
        await_recv(proj_all.at[c, (1 - h) * NX + src_x], px_r.at[2 + k])
    remote(proj_all.at[c], proj_all.at[c], pd_s, pd_r, sibling).start()
    await_recv(proj_all.at[other], pd_r)
    holder = jnp.int32(0)
    for t in range(4 * NX):
        holder = jnp.where(tb_ref[t] == me.t, t, holder)
    own_cols = proj_cols.at[d]
    own_cols[...] = proj_all[lax.rem(holder, 2), holder // 2]
    for k in range(1, NZ):
        remote(own_cols, own_cols, qz_s.at[k - 1], qz_r.at[k - 1], me.at(z=plus(z, k, NZ))).start()

    for j in range(1, NY):
        src_y = plus(y, NY - j, NY)

        @pl.loop(0, NZ)
        def _(k, j=j, src_y=src_y):
            src_d = src_y * NZ + lax.rem(z - k + NZ, NZ)
            await_recv(shard(src_d, c), wy_r.at[(j - 1) * NZ + k])
            to_sibling(src_d, j * NZ + k)

    for k in range(1, NX):
        src_x = plus(x, NX - k, NX)
        await_recv(image(h * NX + src_x), gx_r.at[k - 1])
        await_recv(image((1 - h) * NX + src_x), gx_r.at[2 + k])

    for j in range(NY):
        src_y = plus(y, NY - j, NY)

        @pl.loop(0, NZ)
        def _(k, j=j, src_y=src_y):
            src_d = src_y * NZ + lax.rem(z - k + NZ, NZ)
            await_recv(shard(src_d, other), wd_r.at[j * NZ + k])

    @pl.loop(0, 5)
    def _(n):
        rhs = jnp.concatenate(
            [
                weights[pl.ds(pl.multiple_of(n * 2048, 1024), 1024), :],
                weights[pl.ds(pl.multiple_of(n * 2048 + 1024, 1024), 1024), :],
            ],
            axis=1,
        )
        prod = jnp.dot(grid_img[...], rhs, preferred_element_type=jnp.float32)
        z_ref[2 * n] = prod[:, :128]
        z_ref[2 * n + 1] = prod[:, 128:]

    column = lax.broadcasted_iota(jnp.int32, (GRID, 128), 0)

    def product(tap, gy):
        return z_ref[tap, pl.ds((gy // 3) * SLOT_ROWS + (gy % 3) * GRID, GRID), :]

    for gy in range(0, GRID, 2):
        total = jnp.zeros((GRID, 128), jnp.float32)
        for row_y in (gy, gy + 1):
            parts = []
            for kx in range(3):
                part = None
                for ky in range(3):
                    if 0 <= row_y + ky - 1 < GRID:
                        value = product(3 * ky + kx, row_y + ky - 1)
                        part = value if part is None else part + value
                parts.append(part)
            left = jnp.where(column == 0, 0.0, pltpu.roll(parts[0], 1, 0))
            right = jnp.where(column == GRID - 1, 0.0, pltpu.roll(parts[2], GRID - 1, 0))
            value = parts[1] + left + right
            total = total + product(9, row_y) + value / (1.0 + jnp.exp(-value))
        fs_ref[pl.ds((gy // 2) * GRID, GRID), :] = total
    mean = (fs_ref[pl.ds(0, 144, stride=2), :] + fs_ref[pl.ds(1, 144, stride=2), :]) * 0.25
    own_pool = pooled.at[c, my_slot]
    own_pool[...] = mean.astype(jnp.bfloat16)

    remote(own_pool, own_pool, oz_s, oz_r, flip).start()
    for k in range(1, NX):
        remote(own_pool, own_pool, ox_s.at[k - 1], ox_r.at[k - 1], me.at(x=plus(x, k, NX))).start()

    def cols_to_y(k):
        piece = proj_cols.at[y * NZ + lax.rem(z - k + NZ, NZ)]
        for j in range(1, NY):
            remote(
                piece, piece, qy_s.at[(j - 1) * NZ + k], qy_r.at[(j - 1) * NZ + k], me.at(y=plus(y, j, NY))
            ).start()

    cols_to_y(0)

    @pl.loop(1, NZ)
    def _(k):
        await_recv(proj_cols.at[y * NZ + lax.rem(z - k + NZ, NZ)], qz_r.at[k - 1])
        cols_to_y(k)

    flip_pool = pooled.at[c, flip_slot]
    await_recv(flip_pool, oz_r)
    for k in range(1, NX):
        remote(flip_pool, flip_pool, ox_s.at[2 + k], ox_r.at[2 + k], me.at(x=plus(x, k, NX))).start()

    for j in range(1, NY):
        src_y = plus(y, NY - j, NY)

        @pl.loop(0, NZ)
        def _(k, j=j, src_y=src_y):
            src_d = src_y * NZ + lax.rem(z - k + NZ, NZ)
            await_recv(proj_cols.at[src_d], qy_r.at[(j - 1) * NZ + k])

    for t in range(4 * NX):
        block = tb_ref[t]
        proj_perm[pl.ds(t * 64, 32), :] = proj_cols[2 * block]
        proj_perm[pl.ds(t * 64 + 32, 32), :] = proj_cols[2 * block + 1]

    for k in range(1, NX):
        src_x = plus(x, NX - k, NX)
        await_recv(pooled.at[c, h * NX + src_x], ox_r.at[k - 1])
        await_recv(pooled.at[c, (1 - h) * NX + src_x], ox_r.at[2 + k])
    remote(pooled.at[c], pooled.at[c], od_s, od_r, sibling).start()
    await_recv(pooled.at[other], od_r)

    for slot in range(2):
        index = slot_ref[slot]
        lhs = jnp.concatenate([pooled[index, s] for s in range(SLOTS)], axis=1)
        out_ref[slot] = jnp.dot(lhs, proj_perm[...], preferred_element_type=jnp.float32).astype(jnp.bfloat16)

    ce_conv.wait_send()
    ce_img.wait_send()
    await_send(own_proj, pz_s)
    await_send(own_img, gz_s)
    await_send(own_pool, oz_s)
    await_send(proj_all.at[c], pd_s)
    await_send(pooled.at[c], od_s)
    for k in range(2 * (NX - 1)):
        await_send(own_proj, px_s.at[k])
        await_send(own_img, gx_s.at[k])
        await_send(own_pool, ox_s.at[k])

    @pl.loop(0, NZ - 1)
    def _(k):
        await_send(own_shard, wz_s.at[k])
        await_send(own_cols, qz_s.at[k])

    @pl.loop(0, (NY - 1) * NZ)
    def _(k):
        await_send(own_shard, wy_s.at[k])
        await_send(own_cols, qy_s.at[k])

    @pl.loop(0, NY * NZ)
    def _(k):
        await_send(own_shard, wd_s.at[k])


def per_device(patches, image_slot, trainer_blocks, conv_weight, proj_weight):
    dma = pltpu.SemaphoreType.DMA
    smem = pl.BlockSpec(memory_space=pltpu.SMEM)
    anywhere = pl.BlockSpec(memory_space=pl.ANY)
    bf16, f32 = jnp.bfloat16, jnp.float32
    pairs = [
        dma((2,)),
        dma((NZ - 1,)),
        dma(((NY - 1) * NZ,)),
        dma((NY * NZ,)),
        dma,
        dma((2 * (NX - 1),)),
        dma,
        dma((2 * (NX - 1),)),
        dma,
        dma((NZ - 1,)),
        dma(((NY - 1) * NZ,)),
        dma,
        dma((2 * (NX - 1),)),
        dma,
    ]
    return pl.pallas_call(
        kernel,
        out_shape=jax.ShapeDtypeStruct((2, 144, 512), bf16),
        in_specs=[smem, smem, anywhere, anywhere, anywhere],
        out_specs=pl.BlockSpec(memory_space=pltpu.VMEM),
        scratch_shapes=[
            pltpu.VMEM((2, 36, 1024), bf16),
            pltpu.VMEM((2, 144, 64), bf16),
            pltpu.VMEM((SLOTS * SLOT_ROWS, 1024), bf16),
            pltpu.VMEM((10 * 1024, 128), bf16),
            pltpu.VMEM((10, SLOTS * SLOT_ROWS, 128), f32),
            pltpu.VMEM((288, 128), f32),
            pltpu.VMEM((2, SLOTS, 144, 128), bf16),
            pltpu.VMEM((2, SLOTS, 32, 512), bf16),
            pltpu.VMEM((NY * NZ, 32, 512), bf16),
            pltpu.VMEM((1024, 512), bf16),
            dma((3,)),
        ]
        + [sem for sem in pairs for _ in range(2)],
        compiler_params=pltpu.CompilerParams(
            collective_id=0, has_side_effects=True, vmem_limit_bytes=40 * 1024 * 1024
        ),
        cost_estimate=pl.CostEstimate(flops=2_000_000_000, bytes_accessed=600_000, transcendentals=73728),
        name="vision",
    )(trainer_blocks, image_slot, patches, conv_weight, proj_weight)


def solution(mesh):
    placed = (P("dp", "tp", None), P("dp"), P(), P("dp", "tp"), P("dp", "tp"))
    return jax.shard_map(
        per_device, mesh=mesh, in_specs=placed, out_specs=P("dp", None, "tp"), check_vma=False
    )
```

```python
import functools

import jax
import jax.numpy as jnp
from jax import lax
from jax.experimental import pallas as pl
from jax.experimental.pallas import tpu as pltpu
from jax.sharding import PartitionSpec as P

MESH = pl.DeviceIdType.MESH

GRID = 24
NX, NY, NZ = 4, 4, 8
SLOTS = 2 * NX
SLOT_ROWS = 80
CHIP_ROWS = 72
CUTS = ((0, 48), (48, 32))


class Place:
    def __init__(self):
        d = lax.axis_index("dp")
        t = lax.axis_index("tp")
        self.y, self.z = d // NZ, lax.rem(d, NZ)
        self.h, self.x, self.c = t // (2 * NX), lax.rem(t // 2, NX), lax.rem(t, 2)
        self.d, self.t = d, t
        self.slot = self.h * NX + self.x

    def at(self, y=None, z=None, h=None, x=None, c=None):
        y = self.y if y is None else y
        z = self.z if z is None else z
        h = self.h if h is None else h
        x = self.x if x is None else x
        c = self.c if c is None else c
        return (y * NZ + z, h * (2 * NX) + x * 2 + c)

    def sibling(self):
        return self.at(c=1 - self.c)

    def flip(self):
        return self.at(h=1 - self.h)


def plus(value, step, size):
    return lax.rem(value + step, size)


def kernel(
    tb_ref,
    slot_ref,
    patches,
    conv,
    proj,
    out_ref,
    tokens,
    halves,
    grid_img,
    weights,
    z_ref,
    fs_ref,
    pooled,
    proj_all,
    proj_cols,
    proj_perm,
    result,
    loc,
    ce_s,
    ce_r,
    wz_s,
    wz_r,
    wy_s,
    wy_r,
    wd_s,
    wd_r,
    gz_s,
    gz_r,
    gx_s,
    gx_r,
    pz_s,
    pz_r,
    px_s,
    px_r,
    pd_s,
    pd_r,
    qz_s,
    qz_r,
    qy_s,
    qy_r,
    oz_s,
    oz_r,
    ox_s,
    ox_r,
    od_s,
    od_r,
):
    me = Place()
    c, h, x, y, z, d = me.c, me.h, me.x, me.y, me.z, me.d
    other = 1 - c
    sibling, flip = me.sibling(), me.flip()
    my_slot = me.slot
    flip_slot = (1 - h) * NX + x

    def remote(src, dst, send, recv, where):
        return pltpu.make_async_remote_copy(
            src_ref=src, dst_ref=dst, send_sem=send, recv_sem=recv, device_id=where, device_id_type=MESH
        )

    def await_recv(dst, recv):
        remote(dst, dst, recv, recv, sibling).wait_recv()

    def await_send(src, send):
        remote(src, src, send, send, sibling).wait_send()

    bits = (lax.rem(z, 2), lax.rem(z // 2, 2), z // 4)

    def across(m):
        return sum((1 - bit if m >> i & 1 else bit) * (1 << i) for i, bit in enumerate(bits))

    barrier = pltpu.get_barrier_semaphore()

    def greet(where):
        pl.semaphore_signal(barrier, inc=1, device_id=where, device_id_type=MESH)

    greet(flip)
    for k in range(1, NZ):
        greet(me.at(z=plus(z, k, NZ)))
    for k in range(1, NX):
        greet(me.at(x=plus(x, k, NX)))
    for k in range(1, NY):
        greet(me.at(y=plus(y, k, NY)))
    greet(sibling)

    own_rows = pl.ds(pl.multiple_of(c * 144, 16), 144)
    other_rows = pl.ds(pl.multiple_of(other * 144, 16), 144)
    local = [
        pltpu.make_async_copy(patches.at[c], tokens.at[c], loc.at[0]),
        pltpu.make_async_copy(conv.at[own_rows], halves.at[c], loc.at[1]),
        pltpu.make_async_copy(proj, proj_all.at[c, my_slot], loc.at[2]),
    ]
    for copy in local:
        copy.start()

    row = lax.broadcasted_iota(jnp.int32, (1024, 128), 0)
    lane = lax.broadcasted_iota(jnp.int32, (1024, 128), 1)
    first = tb_ref[2 * my_slot] * 64
    second = tb_ref[2 * my_slot + 1] * 64 - 64
    wanted = lane + jnp.where(lane < 64, first, second)
    weights[pl.ds(9 * 1024, 1024), :] = jnp.where(row == wanted, 1.0, 0.0).astype(jnp.bfloat16)

    for copy in local:
        copy.wait()
    pl.semaphore_wait(barrier, 1 + (NZ - 1) + (NX - 1) + (NY - 1) + 1)

    ce_conv = remote(conv.at[other_rows], halves.at[c], ce_s.at[0], ce_r.at[0], sibling)
    ce_conv.start()
    ce_img = remote(patches.at[other], tokens.at[c], ce_s.at[1], ce_r.at[1], sibling)
    ce_img.start()
    own_proj = proj_all.at[c, my_slot]
    flip_proj = proj_all.at[c, flip_slot]
    remote(own_proj, own_proj, pz_s, pz_r, flip).start()

    def to_x(piece, sends, recvs, first):
        for k in range(1, NX):
            remote(piece, piece, sends.at[first + k - 1], recvs.at[first + k - 1], me.at(x=plus(x, k, NX))).start()

    to_x(own_proj, px_s, px_r, 0)

    def shard(dp, core):
        return weights.at[pl.ds(pl.multiple_of(dp * 288 + core * 144, 16), 144)]

    def w_piece(m, j=0):
        return shard(plus(y, NY - j, NY) * NZ + across(m), c)

    def q_piece(m, j=0):
        return proj_cols.at[plus(y, NY - j, NY) * NZ + across(m)]

    def to_z(piece, m, sends, recvs, partners):
        for p in partners:
            remote(piece(m), piece(m), sends.at[(m ^ p) - 1], recvs.at[(m ^ p) - 1], me.at(z=across(p))).start()

    def to_y(piece, m, sends, recvs):
        for j in range(1, NY):
            i = (j - 1) * NZ + m
            remote(piece(m), piece(m), sends.at[i], recvs.at[i], me.at(y=plus(y, j, NY))).start()

    def w_sibling(m, j=0):
        piece = w_piece(m, j)
        remote(piece, piece, wd_s.at[j * NZ + m], wd_r.at[j * NZ + m], sibling).start()

    def w_step(m, partners):
        if m:
            await_recv(w_piece(m), wz_r.at[m - 1])
        to_z(w_piece, m, wz_s, wz_r, partners)
        to_y(w_piece, m, wy_s, wy_r)
        w_sibling(m)

    def q_step(m, partners):
        if m:
            await_recv(q_piece(m), qz_r.at[m - 1])
        to_z(q_piece, m, qz_s, qz_r, partners)
        to_y(q_piece, m, qy_s, qy_r)

    await_recv(halves.at[other], ce_r.at[0])
    own_shard = w_piece(0)
    own_shard[...] = jnp.concatenate([halves[0], halves[1]], axis=1)
    w_step(0, (4, 2, 1))

    await_recv(tokens.at[other], ce_r.at[1])
    chip_tokens = jnp.concatenate(
        [tokens[0].astype(jnp.float32), tokens[1].astype(jnp.float32), jnp.zeros((SLOT_ROWS - CHIP_ROWS, 1024), jnp.float32)],
        axis=0,
    )

    def image(slot, first=0, count=SLOT_ROWS):
        return grid_img.at[pl.ds(pl.multiple_of(slot * SLOT_ROWS + first, 16), count)]

    image(my_slot)[...] = chip_tokens.astype(jnp.bfloat16)
    for i, cut in enumerate(CUTS):
        remote(image(my_slot, *cut), image(my_slot, *cut), gz_s.at[i], gz_r.at[i], flip).start()
    to_x(image(my_slot), gx_s, gx_r, 0)

    w_step(4, (2, 1))
    w_step(2, (1,))
    w_step(6, (1,))

    await_recv(flip_proj, pz_r)
    to_x(flip_proj, px_s, px_r, NX - 1)

    w_step(1, ())
    w_step(5, ())
    w_step(3, ())
    w_step(7, ())

    for k in range(1, NX):
        src_x = plus(x, NX - k, NX)
        await_recv(proj_all.at[c, h * NX + src_x], px_r.at[k - 1])
        await_recv(proj_all.at[c, (1 - h) * NX + src_x], px_r.at[NX - 1 + k - 1])
    remote(proj_all.at[c], proj_all.at[c], pd_s, pd_r, sibling).start()
    await_recv(proj_all.at[other], pd_r)
    holder = jnp.int32(0)
    for t in range(4 * NX):
        holder = jnp.where(tb_ref[t] == me.t, t, holder)
    q_piece(0)[...] = proj_all[lax.rem(holder, 2), holder // 2]
    q_step(0, (4, 2, 1))

    def image_step(i):
        await_recv(image(flip_slot, *CUTS[i]), gz_r.at[i])
        to_x(image(flip_slot, *CUTS[i]), gx_s, gx_r, (1 + i) * (NX - 1))

    image_step(0)

    for j in range(1, NY):
        for m in range(NZ):
            await_recv(w_piece(m, j), wy_r.at[(j - 1) * NZ + m])
            w_sibling(m, j)

    image_step(1)

    q_step(4, (2, 1))
    q_step(2, (1,))
    q_step(6, (1,))

    for j in range(NY):
        for m in range(NZ):
            dp = plus(y, NY - j, NY) * NZ + across(m)
            await_recv(shard(dp, other), wd_r.at[j * NZ + m])

    for k in range(1, NX):
        src_x = plus(x, NX - k, NX)
        await_recv(image(h * NX + src_x), gx_r.at[k - 1])
        for i, cut in enumerate(CUTS):
            await_recv(image((1 - h) * NX + src_x, *cut), gx_r.at[(1 + i) * (NX - 1) + k - 1])

    @pl.loop(0, 5)
    def _(n):
        rhs = jnp.concatenate(
            [
                weights[pl.ds(pl.multiple_of(n * 2048, 1024), 1024), :],
                weights[pl.ds(pl.multiple_of(n * 2048 + 1024, 1024), 1024), :],
            ],
            axis=1,
        )
        prod = jnp.dot(grid_img[...], rhs, preferred_element_type=jnp.float32)
        z_ref[2 * n] = prod[:, :128]
        z_ref[2 * n + 1] = prod[:, 128:]

    column = lax.broadcasted_iota(jnp.int32, (GRID, 128), 0)

    def product(tap, gy):
        return z_ref[tap, pl.ds((gy // 3) * SLOT_ROWS + (gy % 3) * GRID, GRID), :]

    for gy in range(0, GRID, 2):
        total = jnp.zeros((GRID, 128), jnp.float32)
        for row_y in (gy, gy + 1):
            parts = []
            for kx in range(3):
                part = None
                for ky in range(3):
                    if 0 <= row_y + ky - 1 < GRID:
                        value = product(3 * ky + kx, row_y + ky - 1)
                        part = value if part is None else part + value
                parts.append(part)
            left = jnp.where(column == 0, 0.0, pltpu.roll(parts[0], 1, 0))
            right = jnp.where(column == GRID - 1, 0.0, pltpu.roll(parts[2], GRID - 1, 0))
            value = parts[1] + left + right
            total = total + product(9, row_y) + value / (1.0 + jnp.exp(-value))
        fs_ref[pl.ds((gy // 2) * GRID, GRID), :] = total
    mean = (fs_ref[pl.ds(0, 144, stride=2), :] + fs_ref[pl.ds(1, 144, stride=2), :]) * 0.25
    own_pool = pooled.at[c, my_slot]
    own_pool[...] = mean.astype(jnp.bfloat16)

    remote(own_pool, own_pool, oz_s, oz_r, flip).start()
    to_x(own_pool, ox_s, ox_r, 0)

    q_step(1, ())
    q_step(5, ())
    q_step(3, ())
    q_step(7, ())

    flip_pool = pooled.at[c, flip_slot]
    await_recv(flip_pool, oz_r)
    to_x(flip_pool, ox_s, ox_r, NX - 1)

    for j in range(1, NY):
        for m in range(NZ):
            await_recv(q_piece(m, j), qy_r.at[(j - 1) * NZ + m])

    for t in range(4 * NX):
        block = tb_ref[t]
        proj_perm[pl.ds(t * 64, 32), :] = proj_cols[2 * block]
        proj_perm[pl.ds(t * 64 + 32, 32), :] = proj_cols[2 * block + 1]

    for k in range(1, NX):
        src_x = plus(x, NX - k, NX)
        await_recv(pooled.at[c, h * NX + src_x], ox_r.at[k - 1])
        await_recv(pooled.at[c, (1 - h) * NX + src_x], ox_r.at[NX - 1 + k - 1])
    remote(pooled.at[c], pooled.at[c], od_s, od_r, sibling).start()
    await_recv(pooled.at[other], od_r)

    results = []
    for slot in range(2):
        index = slot_ref[slot]
        lhs = jnp.concatenate([pooled[index, s] for s in range(SLOTS)], axis=1)
        result[slot] = jnp.dot(lhs, proj_perm[...], preferred_element_type=jnp.float32).astype(jnp.bfloat16)
        results.append(pltpu.make_async_copy(result.at[slot], out_ref.at[slot], loc.at[slot]))
        results[-1].start()

    ce_conv.wait_send()
    ce_img.wait_send()
    await_send(own_proj, pz_s)
    for i, cut in enumerate(CUTS):
        await_send(image(my_slot, *cut), gz_s.at[i])
    await_send(own_pool, oz_s)
    await_send(proj_all.at[c], pd_s)
    await_send(pooled.at[c], od_s)
    for k in range(2 * (NX - 1)):
        await_send(own_proj, px_s.at[k])
        await_send(own_pool, ox_s.at[k])
    for k in range(NX - 1):
        await_send(image(my_slot), gx_s.at[k])
        for i, cut in enumerate(CUTS):
            await_send(image(my_slot, *cut), gx_s.at[(1 + i) * (NX - 1) + k])

    @pl.loop(0, NZ - 1)
    def _(k):
        await_send(own_shard, wz_s.at[k])
        await_send(q_piece(0), qz_s.at[k])

    @pl.loop(0, (NY - 1) * NZ)
    def _(k):
        await_send(own_shard, wy_s.at[k])
        await_send(q_piece(0), qy_s.at[k])

    @pl.loop(0, NY * NZ)
    def _(k):
        await_send(own_shard, wd_s.at[k])

    for copy in results:
        copy.wait()


def per_device(patches, image_slot, trainer_blocks, conv_weight, proj_weight):
    dma = pltpu.SemaphoreType.DMA
    smem = pl.BlockSpec(memory_space=pltpu.SMEM)
    anywhere = pl.BlockSpec(memory_space=pl.ANY)
    bf16, f32 = jnp.bfloat16, jnp.float32
    pairs = [
        dma((2,)),
        dma((NZ - 1,)),
        dma(((NY - 1) * NZ,)),
        dma((NY * NZ,)),
        dma((len(CUTS),)),
        dma(((1 + len(CUTS)) * (NX - 1),)),
        dma,
        dma((2 * (NX - 1),)),
        dma,
        dma((NZ - 1,)),
        dma(((NY - 1) * NZ,)),
        dma,
        dma((2 * (NX - 1),)),
        dma,
    ]
    return pl.pallas_call(
        kernel,
        out_shape=jax.ShapeDtypeStruct((2, 144, 512), bf16),
        in_specs=[smem, smem, anywhere, anywhere, anywhere],
        out_specs=anywhere,
        scratch_shapes=[
            pltpu.VMEM((2, 36, 1024), bf16),
            pltpu.VMEM((2, 144, 64), bf16),
            pltpu.VMEM((SLOTS * SLOT_ROWS, 1024), bf16),
            pltpu.VMEM((10 * 1024, 128), bf16),
            pltpu.VMEM((10, SLOTS * SLOT_ROWS, 128), f32),
            pltpu.VMEM((288, 128), f32),
            pltpu.VMEM((2, SLOTS, 144, 128), bf16),
            pltpu.VMEM((2, SLOTS, 32, 512), bf16),
            pltpu.VMEM((NY * NZ, 32, 512), bf16),
            pltpu.VMEM((1024, 512), bf16),
            pltpu.VMEM((2, 144, 512), bf16),
            dma((3,)),
        ]
        + [sem for sem in pairs for _ in range(2)],
        compiler_params=pltpu.CompilerParams(
            collective_id=0, has_side_effects=True, vmem_limit_bytes=40 * 1024 * 1024
        ),
        cost_estimate=pl.CostEstimate(flops=2_000_000_000, bytes_accessed=600_000, transcendentals=73728),
        name="vision",
    )(trainer_blocks, image_slot, patches, conv_weight, proj_weight)


def solution(mesh):
    placed = (P("dp", "tp", None), P("dp"), P(), P("dp", "tp"), P("dp", "tp"))
    return jax.shard_map(
        per_device, mesh=mesh, in_specs=placed, out_specs=P("dp", None, "tp"), check_vma=False
    )
```

```python
import functools

import jax
import jax.numpy as jnp
from jax import lax
from jax.experimental import pallas as pl
from jax.experimental.pallas import tpu as pltpu
from jax.sharding import PartitionSpec as P

MESH = pl.DeviceIdType.MESH

GRID = 24
NX, NY, NZ = 4, 4, 8
SLOTS = 2 * NX
SLOT_ROWS = 80
CHIP_ROWS = 72
CUTS = ((0, 48), (48, 32))


class Place:
    def __init__(self):
        d = lax.axis_index("dp")
        t = lax.axis_index("tp")
        self.y, self.z = d // NZ, lax.rem(d, NZ)
        self.h, self.x, self.c = t // (2 * NX), lax.rem(t // 2, NX), lax.rem(t, 2)
        self.d, self.t = d, t
        self.slot = self.h * NX + self.x

    def at(self, y=None, z=None, h=None, x=None, c=None):
        y = self.y if y is None else y
        z = self.z if z is None else z
        h = self.h if h is None else h
        x = self.x if x is None else x
        c = self.c if c is None else c
        return (y * NZ + z, h * (2 * NX) + x * 2 + c)

    def sibling(self):
        return self.at(c=1 - self.c)

    def flip(self):
        return self.at(h=1 - self.h)


def plus(value, step, size):
    return lax.rem(value + step, size)


def kernel(
    tb_ref,
    slot_ref,
    patches,
    conv,
    proj,
    out_ref,
    tokens,
    halves,
    grid_img,
    weights,
    z_ref,
    fs_ref,
    pooled,
    proj_all,
    proj_cols,
    proj_perm,
    result,
    loc,
    ce_s,
    w_s,
    img_s,
    proj_s,
    proj_cs,
    q_s,
    pool_s,
    pool_cs,
    ce_r,
    wz_r,
    wy_r,
    wd_r,
    gz_r,
    gx_r,
    pz_r,
    px_r,
    pd_r,
    qz_r,
    qy_r,
    oz_r,
    ox_r,
    od_r,
):
    me = Place()
    c, h, x, y, z, d = me.c, me.h, me.x, me.y, me.z, me.d
    other = 1 - c
    sibling, flip = me.sibling(), me.flip()
    my_slot = me.slot
    flip_slot = (1 - h) * NX + x

    def remote(src, dst, send, recv, where):
        return pltpu.make_async_remote_copy(
            src_ref=src, dst_ref=dst, send_sem=send, recv_sem=recv, device_id=where, device_id_type=MESH
        )

    def await_recv(dst, recv):
        remote(dst, dst, recv, recv, sibling).wait_recv()

    def await_send(src, send):
        remote(src, src, send, send, sibling).wait_send()

    bits = (lax.rem(z, 2), lax.rem(z // 2, 2), z // 4)

    def across(m):
        return sum((1 - bit if m >> i & 1 else bit) * (1 << i) for i, bit in enumerate(bits))

    barrier = pltpu.get_barrier_semaphore()

    def greet(where):
        pl.semaphore_signal(barrier, inc=1, device_id=where, device_id_type=MESH)

    greet(flip)
    for k in range(1, NZ):
        greet(me.at(z=plus(z, k, NZ)))
    for k in range(1, NX):
        greet(me.at(x=plus(x, k, NX)))
    for k in range(1, NY):
        greet(me.at(y=plus(y, k, NY)))
    greet(sibling)

    own_rows = pl.ds(pl.multiple_of(c * 144, 16), 144)
    other_rows = pl.ds(pl.multiple_of(other * 144, 16), 144)
    local = [
        pltpu.make_async_copy(patches.at[c], tokens.at[c], loc.at[0]),
        pltpu.make_async_copy(conv.at[own_rows], halves.at[c], loc.at[1]),
        pltpu.make_async_copy(proj, proj_all.at[c, my_slot], loc.at[2]),
    ]
    for copy in local:
        copy.start()

    row = lax.broadcasted_iota(jnp.int32, (1024, 128), 0)
    lane = lax.broadcasted_iota(jnp.int32, (1024, 128), 1)
    first = tb_ref[2 * my_slot] * 64
    second = tb_ref[2 * my_slot + 1] * 64 - 64
    wanted = lane + jnp.where(lane < 64, first, second)
    weights[pl.ds(9 * 1024, 1024), :] = jnp.where(row == wanted, 1.0, 0.0).astype(jnp.bfloat16)

    for copy in local:
        copy.wait()
    pl.semaphore_wait(barrier, 1 + (NZ - 1) + (NX - 1) + (NY - 1) + 1)

    ce_conv = remote(conv.at[other_rows], halves.at[c], ce_s.at[0], ce_r.at[0], sibling)
    ce_conv.start()
    ce_img = remote(patches.at[other], tokens.at[c], ce_s.at[1], ce_r.at[1], sibling)
    ce_img.start()
    own_proj = proj_all.at[c, my_slot]
    flip_proj = proj_all.at[c, flip_slot]

    def to_x(piece, send, recv):
        for k in range(1, NX):
            remote(piece, piece, send, recv, me.at(x=plus(x, k, NX))).start()

    def shard(dp, core):
        return weights.at[pl.ds(pl.multiple_of(dp * 288 + core * 144, 16), 144)]

    def w_piece(m, j=0):
        return shard(plus(y, NY - j, NY) * NZ + across(m), c)

    def q_piece(m, j=0):
        return proj_cols.at[plus(y, NY - j, NY) * NZ + across(m)]

    def to_z(piece, m, send, recvs, partners):
        for p in partners:
            remote(piece(m), piece(m), send, recvs.at[(m ^ p) - 1], me.at(z=across(p))).start()

    def w_to_sibling(m, j):
        remote(w_piece(m, j), w_piece(m, j), w_s, wd_r, sibling).start()

    def w_step(m, partners):
        if m:
            await_recv(w_piece(m), wz_r.at[m - 1])
        to_z(w_piece, m, w_s, wz_r, partners)
        for j in range(1, NY):
            remote(w_piece(m), w_piece(m), w_s, wy_r.at[2 * (j - 1) + m % 2], me.at(y=plus(y, j, NY))).start()
        w_to_sibling(m, 0)

    def w_rest(j, odd):
        await_recv(weights.at[pl.ds(0, 4 * 144)], wy_r.at[2 * (j - 1) + odd])
        for m in range(odd, NZ, 2):
            w_to_sibling(m, j)

    def q_step(m, partners):
        if m:
            await_recv(q_piece(m), qz_r.at[m - 1])
        to_z(q_piece, m, q_s, qz_r, partners)
        for j in range(1, NY):
            remote(q_piece(m), q_piece(m), q_s, qy_r, me.at(y=plus(y, j, NY))).start()

    await_recv(halves.at[other], ce_r.at[0])
    own_shard = w_piece(0)
    own_shard[...] = jnp.concatenate([halves[0], halves[1]], axis=1)
    w_step(0, (4, 2, 1))
    remote(own_proj, own_proj, proj_s, pz_r, flip).start()
    to_x(own_proj, proj_s, px_r)

    await_recv(tokens.at[other], ce_r.at[1])
    chip_tokens = jnp.concatenate(
        [tokens[0].astype(jnp.float32), tokens[1].astype(jnp.float32), jnp.zeros((SLOT_ROWS - CHIP_ROWS, 1024), jnp.float32)],
        axis=0,
    )

    def image(slot, first=0, count=SLOT_ROWS):
        return grid_img.at[pl.ds(pl.multiple_of(slot * SLOT_ROWS + first, 16), count)]

    image(my_slot)[...] = chip_tokens.astype(jnp.bfloat16)
    to_x(image(my_slot), img_s, gx_r.at[0])

    def flip_cut(i):
        piece = image(my_slot, *CUTS[i])
        remote(piece, piece, img_s, gz_r.at[i], flip).start()

    def image_step(i):
        piece = image(flip_slot, *CUTS[i])
        await_recv(piece, gz_r.at[i])
        to_x(piece, img_s, gx_r.at[1])

    def multiply(half):
        rows = pl.ds(pl.multiple_of(half * (NX * SLOT_ROWS), 64), NX * SLOT_ROWS)

        @pl.loop(0, 5)
        def _(n):
            rhs = jnp.concatenate(
                [
                    weights[pl.ds(pl.multiple_of(n * 2048, 1024), 1024), :],
                    weights[pl.ds(pl.multiple_of(n * 2048 + 1024, 1024), 1024), :],
                ],
                axis=1,
            )
            prod = jnp.dot(grid_img[rows, :], rhs, preferred_element_type=jnp.float32)
            z_ref[2 * n, rows, :] = prod[:, :128]
            z_ref[2 * n + 1, rows, :] = prod[:, 128:]

    flip_cut(0)
    w_step(4, (2, 1))
    flip_cut(1)
    w_step(2, (1,))
    w_step(6, (1,))
    await_recv(flip_proj, pz_r)
    to_x(flip_proj, proj_s, px_r)
    w_step(1, ())
    w_step(5, ())
    await_recv(proj_all.at[c, pl.ds(0, 2 * (NX - 1))], px_r)
    remote(proj_all.at[c], proj_all.at[c], proj_cs, pd_r, sibling).start()
    w_step(3, ())
    w_step(7, ())
    await_recv(proj_all.at[other], pd_r)
    holder = jnp.int32(0)
    for t in range(4 * NX):
        holder = jnp.where(tb_ref[t] == me.t, t, holder)
    q_piece(0)[...] = proj_all[lax.rem(holder, 2), holder // 2]
    q_step(0, (4, 2, 1))

    image_step(0)
    for j in range(1, NY):
        w_rest(j, 0)
    for j in range(1, NY):
        w_rest(j, 1)
    image_step(1)
    q_step(4, (2, 1))
    await_recv(weights.at[pl.ds(0, NY * NZ * 144)], wd_r)
    await_recv(grid_img.at[pl.ds(0, (NX - 1) * SLOT_ROWS)], gx_r.at[0])
    multiply(h)
    q_step(2, (1,))
    q_step(6, (1,))
    await_recv(grid_img.at[pl.ds(0, (NX - 1) * SLOT_ROWS)], gx_r.at[1])
    multiply(1 - h)

    column = lax.broadcasted_iota(jnp.int32, (GRID, 128), 0)

    def product(tap, gy):
        return z_ref[tap, pl.ds((gy // 3) * SLOT_ROWS + (gy % 3) * GRID, GRID), :]

    for gy in range(0, GRID, 2):
        total = jnp.zeros((GRID, 128), jnp.float32)
        for row_y in (gy, gy + 1):
            parts = []
            for kx in range(3):
                part = None
                for ky in range(3):
                    if 0 <= row_y + ky - 1 < GRID:
                        value = product(3 * ky + kx, row_y + ky - 1)
                        part = value if part is None else part + value
                parts.append(part)
            left = jnp.where(column == 0, 0.0, pltpu.roll(parts[0], 1, 0))
            right = jnp.where(column == GRID - 1, 0.0, pltpu.roll(parts[2], GRID - 1, 0))
            value = parts[1] + left + right
            total = total + product(9, row_y) + value / (1.0 + jnp.exp(-value))
        fs_ref[pl.ds((gy // 2) * GRID, GRID), :] = total
    mean = (fs_ref[pl.ds(0, 144, stride=2), :] + fs_ref[pl.ds(1, 144, stride=2), :]) * 0.25
    own_pool = pooled.at[c, my_slot]
    own_pool[...] = mean.astype(jnp.bfloat16)

    remote(own_pool, own_pool, pool_s, oz_r, flip).start()
    to_x(own_pool, pool_s, ox_r)
    for m in (1, 5, 3, 7):
        q_step(m, ())
    flip_pool = pooled.at[c, flip_slot]
    await_recv(flip_pool, oz_r)
    to_x(flip_pool, pool_s, ox_r)
    await_recv(proj_cols.at[pl.ds(0, (NY - 1) * NZ)], qy_r)

    for t in range(4 * NX):
        block = tb_ref[t]
        proj_perm[pl.ds(t * 64, 32), :] = proj_cols[2 * block]
        proj_perm[pl.ds(t * 64 + 32, 32), :] = proj_cols[2 * block + 1]

    await_recv(pooled.at[c, pl.ds(0, 2 * (NX - 1))], ox_r)
    remote(pooled.at[c], pooled.at[c], pool_cs, od_r, sibling).start()
    await_recv(pooled.at[other], od_r)

    results = []
    for slot in range(2):
        index = slot_ref[slot]
        lhs = jnp.concatenate([pooled[index, s] for s in range(SLOTS)], axis=1)
        result[slot] = jnp.dot(lhs, proj_perm[...], preferred_element_type=jnp.float32).astype(jnp.bfloat16)
        results.append(pltpu.make_async_copy(result.at[slot], out_ref.at[slot], loc.at[slot]))
        results[-1].start()

    ce_conv.wait_send()
    ce_img.wait_send()
    await_send(weights.at[pl.ds(0, (NZ - 1 + (NY - 1) * NZ + NY * NZ) * 144)], w_s)
    await_send(grid_img.at[pl.ds(0, (2 * (NX - 1) + 1) * SLOT_ROWS)], img_s)
    await_send(proj_all.at[c, pl.ds(0, 2 * (NX - 1) + 1)], proj_s)
    await_send(proj_all.at[c], proj_cs)
    await_send(proj_cols.at[pl.ds(0, NZ - 1 + (NY - 1) * NZ)], q_s)
    await_send(pooled.at[c, pl.ds(0, 2 * (NX - 1) + 1)], pool_s)
    await_send(pooled.at[c], pool_cs)
    for copy in results:
        copy.wait()


def per_device(patches, image_slot, trainer_blocks, conv_weight, proj_weight):
    dma = pltpu.SemaphoreType.DMA
    smem = pl.BlockSpec(memory_space=pltpu.SMEM)
    anywhere = pl.BlockSpec(memory_space=pl.ANY)
    bf16, f32 = jnp.bfloat16, jnp.float32
    sems = [
        dma((2,)),
        dma,
        dma,
        dma,
        dma,
        dma,
        dma,
        dma,
        dma((2,)),
        dma((NZ - 1,)),
        dma((2 * (NY - 1),)),
        dma,
        dma((len(CUTS),)),
        dma((2,)),
        dma,
        dma,
        dma,
        dma((NZ - 1,)),
        dma,
        dma,
        dma,
        dma,
    ]
    return pl.pallas_call(
        kernel,
        out_shape=jax.ShapeDtypeStruct((2, 144, 512), bf16),
        in_specs=[smem, smem, anywhere, anywhere, anywhere],
        out_specs=anywhere,
        scratch_shapes=[
            pltpu.VMEM((2, 36, 1024), bf16),
            pltpu.VMEM((2, 144, 64), bf16),
            pltpu.VMEM((SLOTS * SLOT_ROWS, 1024), bf16),
            pltpu.VMEM((10 * 1024, 128), bf16),
            pltpu.VMEM((10, SLOTS * SLOT_ROWS, 128), f32),
            pltpu.VMEM((288, 128), f32),
            pltpu.VMEM((2, SLOTS, 144, 128), bf16),
            pltpu.VMEM((2, SLOTS, 32, 512), bf16),
            pltpu.VMEM((NY * NZ, 32, 512), bf16),
            pltpu.VMEM((1024, 512), bf16),
            pltpu.VMEM((2, 144, 512), bf16),
            dma((3,)),
        ]
        + sems,
        compiler_params=pltpu.CompilerParams(
            collective_id=0, has_side_effects=True, vmem_limit_bytes=40 * 1024 * 1024
        ),
        cost_estimate=pl.CostEstimate(flops=2_000_000_000, bytes_accessed=600_000, transcendentals=73728),
        name="vision",
    )(trainer_blocks, image_slot, patches, conv_weight, proj_weight)


def solution(mesh):
    placed = (P("dp", "tp", None), P("dp"), P(), P("dp", "tp"), P("dp", "tp"))
    return jax.shard_map(
        per_device, mesh=mesh, in_specs=placed, out_specs=P("dp", None, "tp"), check_vma=False
    )
```

```python
import functools

import jax
import jax.numpy as jnp
from jax import lax
from jax.experimental import pallas as pl
from jax.experimental.pallas import tpu as pltpu
from jax.sharding import PartitionSpec as P

MESH = pl.DeviceIdType.MESH

GRID = 24
NX, NY, NZ = 4, 4, 8
SLOTS = 2 * NX
SLOT_ROWS = 80
CHIP_ROWS = 72
BODY_ROWS = 64
CUTS = ((0, 32), (32, 32))


class Place:
    def __init__(self):
        d = lax.axis_index("dp")
        t = lax.axis_index("tp")
        self.y, self.z = d // NZ, lax.rem(d, NZ)
        self.h, self.x, self.c = t // (2 * NX), lax.rem(t // 2, NX), lax.rem(t, 2)
        self.d, self.t = d, t
        self.slot = self.h * NX + self.x

    def at(self, y=None, z=None, h=None, x=None, c=None):
        y = self.y if y is None else y
        z = self.z if z is None else z
        h = self.h if h is None else h
        x = self.x if x is None else x
        c = self.c if c is None else c
        return (y * NZ + z, h * (2 * NX) + x * 2 + c)

    def sibling(self):
        return self.at(c=1 - self.c)

    def flip(self):
        return self.at(h=1 - self.h)


def plus(value, step, size):
    return lax.rem(value + step, size)


def kernel(
    tb_in,
    slot_in,
    patches,
    conv,
    proj,
    out_ref,
    tb_ref,
    slot_ref,
    tokens,
    halves,
    pair_rows,
    grid_img,
    rests,
    weights,
    z_ref,
    fs_ref,
    pooled,
    proj_all,
    proj_cols,
    proj_perm,
    own_pool,
    result,
    loc,
    ce_s,
    w_s,
    img_s,
    rest_s,
    proj_s,
    proj_cs,
    q_s,
    pool_s,
    pool_cs,
    ce_r,
    wz_r,
    wy_r,
    wd_r,
    gz_r,
    gx_r,
    rz_r,
    rx_r,
    pz_r,
    px_r,
    pd_r,
    qz_r,
    qy_r,
    oz_r,
    ox_r,
    oc_r,
    od_r,
):
    me = Place()
    c, h, x, y, z, d = me.c, me.h, me.x, me.y, me.z, me.d
    other = 1 - c
    sibling, flip = me.sibling(), me.flip()
    my_slot = me.slot
    flip_slot = (1 - h) * NX + x

    def remote(src, dst, send, recv, where):
        return pltpu.make_async_remote_copy(
            src_ref=src, dst_ref=dst, send_sem=send, recv_sem=recv, device_id=where, device_id_type=MESH
        )

    def await_recv(dst, recv):
        remote(dst, dst, recv, recv, sibling).wait_recv()

    def await_send(src, send):
        remote(src, src, send, send, sibling).wait_send()

    bits = (lax.rem(z, 2), lax.rem(z // 2, 2), z // 4)

    def across(m):
        return sum((1 - bit if m >> i & 1 else bit) * (1 << i) for i, bit in enumerate(bits))

    barrier = pltpu.get_barrier_semaphore()

    def greet(where):
        pl.semaphore_signal(barrier, inc=1, device_id=where, device_id_type=MESH)

    greet(flip)
    greet(me.at(h=1 - h, c=other))
    for k in range(1, NZ):
        greet(me.at(z=plus(z, k, NZ)))
    for k in range(1, NX):
        greet(me.at(x=plus(x, k, NX)))
        greet(me.at(x=plus(x, k, NX), c=other))
    for k in range(1, NY):
        greet(me.at(y=plus(y, k, NY)))
    greet(sibling)

    local = [
        pltpu.make_async_copy(patches, tokens.at[c], loc.at[0]),
        pltpu.make_async_copy(conv, halves.at[c], loc.at[1]),
        pltpu.make_async_copy(proj, proj_all.at[c, my_slot], loc.at[2]),
        pltpu.make_async_copy(tb_in, tb_ref, loc.at[3]),
        pltpu.make_async_copy(slot_in, slot_ref, loc.at[4]),
    ]
    for copy in local:
        copy.start()

    for copy in local:
        copy.wait()
    pl.semaphore_wait(barrier, 2 + (NZ - 1) + 2 * (NX - 1) + (NY - 1) + 1)

    ce_conv = remote(halves.at[c], halves.at[c], ce_s.at[0], ce_r.at[0], sibling)
    ce_conv.start()
    ce_img = remote(tokens.at[c], tokens.at[c], ce_s.at[1], ce_r.at[1], sibling)
    ce_img.start()
    own_proj = proj_all.at[c, my_slot]
    flip_proj = proj_all.at[c, flip_slot]

    def to_x(piece, send, recv):
        for k in range(1, NX):
            remote(piece, piece, send, recv, me.at(x=plus(x, k, NX))).start()

    def shard(dp, core):
        return weights.at[pl.ds(pl.multiple_of(dp * 288 + core * 144, 16), 144)]

    def w_piece(m, j=0):
        return shard(plus(y, NY - j, NY) * NZ + across(m), c)

    def q_piece(m, j=0):
        return proj_cols.at[plus(y, NY - j, NY) * NZ + across(m)]

    def to_z(piece, m, send, recvs, partners):
        for p in partners:
            remote(piece(m), piece(m), send, recvs.at[(m ^ p) - 1], me.at(z=across(p))).start()

    def w_to_sibling(m, j):
        remote(w_piece(m, j), w_piece(m, j), w_s, wd_r, sibling).start()

    def w_step(m, partners):
        if m:
            await_recv(w_piece(m), wz_r.at[m - 1])
        to_z(w_piece, m, w_s, wz_r, partners)
        for j in range(1, NY):
            remote(w_piece(m), w_piece(m), w_s, wy_r.at[2 * (j - 1) + m % 2], me.at(y=plus(y, j, NY))).start()
        w_to_sibling(m, 0)

    def w_rest(j, odd):
        await_recv(weights.at[pl.ds(0, 4 * 144)], wy_r.at[2 * (j - 1) + odd])
        for m in range(odd, NZ, 2):
            w_to_sibling(m, j)

    def q_step(m, partners):
        if m:
            await_recv(q_piece(m), qz_r.at[m - 1])
        to_z(q_piece, m, q_s, qz_r, partners)
        for j in range(1, NY):
            remote(q_piece(m), q_piece(m), q_s, qy_r, me.at(y=plus(y, j, NY))).start()

    await_recv(halves.at[other], ce_r.at[0])
    own_shard = w_piece(0)
    both = jnp.concatenate([halves[0], halves[1]], axis=0).astype(jnp.float32)
    both = jnp.concatenate([both, jnp.zeros((128, 96), jnp.float32)], axis=1)
    pair_rows[...] = both.T[:288].astype(jnp.bfloat16)
    own_shard[...] = pair_rows[pl.ds(pl.multiple_of(c * 144, 16), 144), :]
    w_step(0, (4, 2, 1))
    remote(own_proj, own_proj, proj_s, pz_r, flip).start()
    to_x(own_proj, proj_s, px_r)

    await_recv(tokens.at[other], ce_r.at[1])
    mine = [
        jnp.where(c == 0, both[:, 0, :], both[:, 1, :]) for both in (tokens[i].astype(jnp.float32) for i in range(2))
    ]
    chip_tokens = jnp.concatenate(mine + [jnp.zeros((SLOT_ROWS - CHIP_ROWS, 1024), jnp.float32)], axis=0)

    def image(slot, first=0, count=SLOT_ROWS):
        return grid_img.at[pl.ds(pl.multiple_of(slot * SLOT_ROWS + first, 16), count)]

    image(my_slot, 0, BODY_ROWS)[...] = chip_tokens[:BODY_ROWS].astype(jnp.bfloat16)
    own_rest = chip_tokens[BODY_ROWS:CHIP_ROWS]
    rests[my_slot] = jnp.concatenate([own_rest[:, :512], own_rest[:, 512:]], axis=0).astype(jnp.bfloat16)
    to_x(image(my_slot, 0, BODY_ROWS), img_s, gx_r.at[0])
    to_x(rests.at[my_slot], rest_s, rx_r.at[0])

    def flip_cut(i):
        piece = image(my_slot, *CUTS[i])
        remote(piece, piece, img_s, gz_r.at[i], flip).start()

    def flip_rest():
        remote(rests.at[my_slot], rests.at[my_slot], rest_s, rz_r, flip).start()

    def image_step(i):
        piece = image(flip_slot, *CUTS[i])
        await_recv(piece, gz_r.at[i])
        to_x(piece, img_s, gx_r.at[1])

    def rest_step():
        await_recv(rests.at[flip_slot], rz_r)
        to_x(rests.at[flip_slot], rest_s, rx_r.at[1])

    def image_wait(which):
        await_recv(grid_img.at[pl.ds(0, (NX - 1) * BODY_ROWS)], gx_r.at[which])
        await_recv(rests.at[pl.ds(0, NX - 1)], rx_r.at[which])

    def put_rests(half):
        for i in range(NX):
            rest = rests[half * NX + i].astype(jnp.float32)
            rest = jnp.concatenate([rest[:8], rest[8:]], axis=1)
            rest = jnp.concatenate([rest, jnp.zeros((8, 1024), jnp.float32)], axis=0)
            image(half * NX + i, BODY_ROWS, 16)[...] = rest.astype(jnp.bfloat16)

    def multiply(half):
        put_rests(half)
        rows = pl.ds(pl.multiple_of(half * (NX * SLOT_ROWS), 64), NX * SLOT_ROWS)

        @pl.loop(0, 5)
        def _(n):
            rhs = jnp.concatenate(
                [
                    weights[pl.ds(pl.multiple_of(n * 2048, 1024), 1024), :],
                    weights[pl.ds(pl.multiple_of(n * 2048 + 1024, 1024), 1024), :],
                ],
                axis=1,
            )
            prod = jnp.dot(grid_img[rows, :], rhs, preferred_element_type=jnp.float32)
            z_ref[2 * n, rows, :] = prod[:, :128]
            z_ref[2 * n + 1, rows, :] = prod[:, 128:]

    flip_cut(0)
    row = lax.broadcasted_iota(jnp.int32, (1024, 128), 0)
    lane = lax.broadcasted_iota(jnp.int32, (1024, 128), 1)
    first = tb_ref[2 * my_slot] * 64
    second = tb_ref[2 * my_slot + 1] * 64 - 64
    wanted = lane + jnp.where(lane < 64, first, second)
    weights[pl.ds(9 * 1024, 1024), :] = jnp.where(row == wanted, 1.0, 0.0).astype(jnp.bfloat16)
    w_step(4, (2, 1))
    flip_cut(1)
    flip_rest()
    w_step(2, (1,))
    w_step(6, (1,))
    await_recv(flip_proj, pz_r)
    to_x(flip_proj, proj_s, px_r)
    w_step(1, ())
    w_step(5, ())
    await_recv(proj_all.at[c, pl.ds(0, 2 * (NX - 1))], px_r)
    remote(proj_all.at[c], proj_all.at[c], proj_cs, pd_r, sibling).start()
    w_step(3, ())
    w_step(7, ())
    await_recv(proj_all.at[other], pd_r)
    holder = jnp.int32(0)
    for t in range(4 * NX):
        holder = jnp.where(tb_ref[t] == me.t, t, holder)
    q_piece(0)[...] = proj_all[lax.rem(holder, 2), holder // 2]
    q_step(0, (4, 2, 1))

    image_step(0)
    for j in range(1, NY):
        w_rest(j, 0)
    image_step(1)
    rest_step()
    for j in range(1, NY):
        w_rest(j, 1)
    q_step(4, (2, 1))
    await_recv(weights.at[pl.ds(0, NY * NZ * 144)], wd_r)
    image_wait(0)
    multiply(h)
    q_step(2, (1,))
    q_step(6, (1,))
    image_wait(1)
    multiply(1 - h)

    column = lax.broadcasted_iota(jnp.int32, (GRID, 128), 0)

    def product(tap, gy):
        return z_ref[tap, pl.ds((gy // 3) * SLOT_ROWS + (gy % 3) * GRID, GRID), :]

    for gy in range(0, GRID, 2):
        total = jnp.zeros((GRID, 128), jnp.float32)
        for row_y in (gy, gy + 1):
            parts = []
            for kx in range(3):
                part = None
                for ky in range(3):
                    if 0 <= row_y + ky - 1 < GRID:
                        value = product(3 * ky + kx, row_y + ky - 1)
                        part = value if part is None else part + value
                parts.append(part)
            left = jnp.where(column == 0, 0.0, pltpu.roll(parts[0], 1, 0))
            right = jnp.where(column == GRID - 1, 0.0, pltpu.roll(parts[2], GRID - 1, 0))
            value = parts[1] + left + right
            total = total + product(9, row_y) + value / (1.0 + jnp.exp(-value))
        fs_ref[pl.ds((gy // 2) * GRID, GRID), :] = total
    mean = (fs_ref[pl.ds(0, 144, stride=2), :] + fs_ref[pl.ds(1, 144, stride=2), :]) * 0.25
    own_pool[...] = mean.astype(jnp.bfloat16)

    def pool_to_x(piece, dst):
        for k in range(1, NX):
            remote(piece, dst, pool_s, ox_r, me.at(x=plus(x, k, NX), c=1)).start()

    remote(own_pool, pooled.at[c, my_slot], pool_s, oz_r.at[c], me.at(h=1 - h, c=1)).start()
    pool_to_x(own_pool, pooled.at[c, my_slot])

    @pl.when(c == 0)
    def _():
        remote(own_pool, pooled.at[0, my_slot], pool_cs, oc_r, sibling).start()

    @pl.when(c == 1)
    def _():
        pooled[1, my_slot] = own_pool[...]

    for m in (1, 5, 3, 7):
        q_step(m, ())
    @pl.when(c == 1)
    def _():
        for i in (1, 0):
            flip_pool = pooled.at[i, flip_slot]
            await_recv(flip_pool, oz_r.at[i])
            pool_to_x(flip_pool, flip_pool)

    await_recv(proj_cols.at[pl.ds(0, (NY - 1) * NZ)], qy_r)

    for t in range(4 * NX):
        block = tb_ref[t]
        proj_perm[pl.ds(t * 64, 32), :] = proj_cols[2 * block]
        proj_perm[pl.ds(t * 64 + 32, 32), :] = proj_cols[2 * block + 1]

    @pl.when(c == 1)
    def _():
        await_recv(pooled.at[0, my_slot], oc_r)
        await_recv(pooled.at[:, pl.ds(0, 2 * (NX - 1))], ox_r)
        remote(pooled, pooled, pool_cs, od_r, sibling).start()

    @pl.when(c == 0)
    def _():
        await_recv(pooled, od_r)

    def project(img):
        lhs = jnp.concatenate([pooled[img, s] for s in range(SLOTS)], axis=1)
        return jnp.dot(lhs, proj_perm[...], preferred_element_type=jnp.float32).astype(jnp.bfloat16)

    results = []
    for slot in range(2):
        result[slot] = project(slot_ref[slot])
        results.append(pltpu.make_async_copy(result.at[slot], out_ref.at[slot], loc.at[slot]))
        results[-1].start()

    ce_conv.wait_send()
    ce_img.wait_send()
    await_send(weights.at[pl.ds(0, (NZ - 1 + (NY - 1) * NZ + NY * NZ) * 144)], w_s)
    await_send(grid_img.at[pl.ds(0, (2 * (NX - 1) + 1) * BODY_ROWS)], img_s)
    await_send(rests.at[pl.ds(0, 2 * (NX - 1) + 1)], rest_s)
    await_send(proj_all.at[c, pl.ds(0, 2 * (NX - 1) + 1)], proj_s)
    await_send(proj_all.at[c], proj_cs)
    await_send(proj_cols.at[pl.ds(0, NZ - 1 + (NY - 1) * NZ)], q_s)
    @pl.when(c == 0)
    def _():
        await_send(pooled.at[0, pl.ds(0, NX)], pool_s)
        await_send(own_pool, pool_cs)

    @pl.when(c == 1)
    def _():
        await_send(pooled.at[:, pl.ds(0, (3 * (NX - 1) + 1) // 2)], pool_s)
        await_send(pooled, pool_cs)

    for copy in results:
        copy.wait()


def per_device(patches, image_slot, trainer_blocks, conv_weight, proj_weight):
    dma = pltpu.SemaphoreType.DMA
    anywhere = pl.BlockSpec(memory_space=pl.ANY)
    bf16, f32 = jnp.bfloat16, jnp.float32
    sems = [
        dma((2,)),
        dma,
        dma,
        dma,
        dma,
        dma,
        dma,
        dma,
        dma,
        dma((2,)),
        dma((NZ - 1,)),
        dma((2 * (NY - 1),)),
        dma,
        dma((len(CUTS),)),
        dma((2,)),
        dma,
        dma((2,)),
        dma,
        dma,
        dma,
        dma((NZ - 1,)),
        dma,
        dma((2,)),
        dma,
        dma,
        dma,
    ]
    return pl.pallas_call(
        kernel,
        out_shape=jax.ShapeDtypeStruct((2, 144, 512), bf16),
        in_specs=[pl.BlockSpec(memory_space=pltpu.HBM)] * 5,
        out_specs=anywhere,
        scratch_shapes=[
            pltpu.SMEM((16,), jnp.int32),
            pltpu.SMEM((2,), jnp.int32),
            pltpu.VMEM((2, 36, 2, 1024), bf16),
            pltpu.VMEM((2, 64, 288), bf16),
            pltpu.VMEM((288, 128), bf16),
            pltpu.VMEM((SLOTS * SLOT_ROWS, 1024), bf16),
            pltpu.VMEM((SLOTS, 16, 512), bf16),
            pltpu.VMEM((10 * 1024, 128), bf16),
            pltpu.VMEM((10, SLOTS * SLOT_ROWS, 128), f32),
            pltpu.VMEM((288, 128), f32),
            pltpu.VMEM((2, SLOTS, 144, 128), bf16),
            pltpu.VMEM((2, SLOTS, 32, 512), bf16),
            pltpu.VMEM((NY * NZ, 32, 512), bf16),
            pltpu.VMEM((1024, 512), bf16),
            pltpu.VMEM((144, 128), bf16),
            pltpu.VMEM((2, 144, 512), bf16),
            dma((5,)),
        ]
        + sems,
        compiler_params=pltpu.CompilerParams(
            collective_id=0, has_side_effects=True, vmem_limit_bytes=40 * 1024 * 1024
        ),
        cost_estimate=pl.CostEstimate(flops=2_000_000_000, bytes_accessed=600_000, transcendentals=73728),
        name="vision",
    )(*(pltpu.with_memory_space_constraint(a, pltpu.HBM) for a in (trainer_blocks, image_slot, jnp.transpose(patches, (1, 0, 2)), conv_weight.T, proj_weight)))


def solution(mesh):
    placed = (P("dp", "tp", None), P("dp"), P(), P("dp", "tp"), P("dp", "tp"))
    return jax.shard_map(
        per_device, mesh=mesh, in_specs=placed, out_specs=P("dp", None, "tp"), check_vma=False
    )
```

```python
import functools

import jax
import jax.numpy as jnp
from jax import lax
from jax.experimental import pallas as pl
from jax.experimental.pallas import tpu as pltpu
from jax.sharding import PartitionSpec as P

MESH = pl.DeviceIdType.MESH

GRID = 24
NX, NY, NZ = 4, 4, 8
SLOTS = 2 * NX
SLOT_ROWS = 80
CHIP_ROWS = 72
BODY_ROWS = 64
CUTS = ((0, 32), (32, 32))


class Place:
    def __init__(self):
        d = lax.axis_index("dp")
        t = lax.axis_index("tp")
        self.y, self.z = d // NZ, lax.rem(d, NZ)
        self.h, self.x, self.c = t // (2 * NX), lax.rem(t // 2, NX), lax.rem(t, 2)
        self.d, self.t = d, t
        self.slot = self.h * NX + self.x

    def at(self, y=None, z=None, h=None, x=None, c=None):
        y = self.y if y is None else y
        z = self.z if z is None else z
        h = self.h if h is None else h
        x = self.x if x is None else x
        c = self.c if c is None else c
        return (y * NZ + z, h * (2 * NX) + x * 2 + c)

    def sibling(self):
        return self.at(c=1 - self.c)

    def flip(self):
        return self.at(h=1 - self.h)


def plus(value, step, size):
    return lax.rem(value + step, size)


def kernel(
    tb_in,
    slot_in,
    patches,
    conv,
    proj,
    out_ref,
    tb_ref,
    slot_ref,
    tokens,
    halves,
    pair_rows,
    grid_img,
    rests,
    weights,
    z_ref,
    fs_ref,
    pooled,
    proj_all,
    proj_cols,
    proj_perm,
    own_pool,
    result,
    half_ok,
    flip_ok,
    loc,
    ce_s,
    w_s,
    img_s,
    rest_s,
    proj_s,
    proj_cs,
    q_s,
    pool_s,
    pool_cs,
    ce_r,
    wz_r,
    wy_r,
    wd_r,
    gz_r,
    gx_r,
    rz_r,
    rx_r,
    pz_r,
    px_r,
    pd_r,
    qz_r,
    qy_r,
    oz_r,
    ox_r,
    oc_r,
    od_r,
):
    me = Place()
    c, h, x, y, z, d = me.c, me.h, me.x, me.y, me.z, me.d
    other = 1 - c
    sibling, flip = me.sibling(), me.flip()
    my_slot = me.slot
    flip_slot = (1 - h) * NX + x

    def remote(src, dst, send, recv, where):
        return pltpu.make_async_remote_copy(
            src_ref=src, dst_ref=dst, send_sem=send, recv_sem=recv, device_id=where, device_id_type=MESH
        )

    def await_recv(dst, recv):
        remote(dst, dst, recv, recv, sibling).wait_recv()

    def await_send(src, send):
        remote(src, src, send, send, sibling).wait_send()

    bits = (lax.rem(z, 2), lax.rem(z // 2, 2), z // 4)

    def across(m):
        return sum((1 - bit if m >> i & 1 else bit) * (1 << i) for i, bit in enumerate(bits))

    barrier = pltpu.get_barrier_semaphore()

    def greet(where):
        pl.semaphore_signal(barrier, inc=1, device_id=where, device_id_type=MESH)

    for k in range(1, NZ):
        greet(me.at(z=plus(z, k, NZ), c=1))
    for k in range(1, NX):
        greet(me.at(x=plus(x, k, NX), c=1))
    for k in range(1, NY):
        greet(me.at(y=plus(y, k, NY), c=1))

    @pl.when(c == 0)
    def _():
        greet(sibling)

    greet(me.at(h=1 - h, c=0))

    local = [
        pltpu.make_async_copy(patches, tokens.at[c], loc.at[0]),
        pltpu.make_async_copy(conv, halves.at[c], loc.at[1]),
        pltpu.make_async_copy(proj, proj_all.at[c, my_slot], loc.at[2]),
        pltpu.make_async_copy(tb_in, tb_ref, loc.at[3]),
        pltpu.make_async_copy(slot_in, slot_ref, loc.at[4]),
    ]
    for copy in local:
        copy.start()

    for copy in local:
        copy.wait()
    @pl.when(c == 1)
    def _():
        pl.semaphore_wait(barrier, 2 * (NZ - 1 + NX - 1 + NY - 1) + 1)
        pl.semaphore_signal(half_ok, inc=1, device_id=sibling, device_id_type=MESH)

    @pl.when(c == 0)
    def _():
        pl.semaphore_wait(half_ok, 1)

    def meet_other_half():
        @pl.when(c == 0)
        def _():
            pl.semaphore_wait(barrier, 2)
            pl.semaphore_signal(flip_ok, inc=1, device_id=sibling, device_id_type=MESH)

        @pl.when(c == 1)
        def _():
            pl.semaphore_wait(flip_ok, 1)


    ce_conv = remote(halves.at[c], halves.at[c], ce_s.at[0], ce_r.at[0], sibling)
    ce_conv.start()
    ce_img = remote(tokens.at[c], tokens.at[c], ce_s.at[1], ce_r.at[1], sibling)
    ce_img.start()
    own_proj = proj_all.at[c, my_slot]
    flip_proj = proj_all.at[c, flip_slot]

    def to_x(piece, send, recv):
        for k in range(1, NX):
            remote(piece, piece, send, recv, me.at(x=plus(x, k, NX))).start()

    def shard(dp, core):
        return weights.at[pl.ds(pl.multiple_of(dp * 288 + core * 144, 16), 144)]

    def w_piece(m, j=0):
        return shard(plus(y, NY - j, NY) * NZ + across(m), c)

    def q_piece(m, j=0):
        return proj_cols.at[plus(y, NY - j, NY) * NZ + across(m)]

    def to_z(piece, m, send, recvs, partners):
        for p in partners:
            remote(piece(m), piece(m), send, recvs.at[(m ^ p) - 1], me.at(z=across(p))).start()

    def w_to_sibling(m, j):
        remote(w_piece(m, j), w_piece(m, j), w_s, wd_r, sibling).start()

    def w_step(m, partners):
        if m:
            await_recv(w_piece(m), wz_r.at[m - 1])
        to_z(w_piece, m, w_s, wz_r, partners)
        for j in range(1, NY):
            remote(w_piece(m), w_piece(m), w_s, wy_r.at[2 * (j - 1) + m % 2], me.at(y=plus(y, j, NY))).start()
        w_to_sibling(m, 0)

    def w_rest(j, odd):
        await_recv(weights.at[pl.ds(0, 4 * 144)], wy_r.at[2 * (j - 1) + odd])
        for m in range(odd, NZ, 2):
            w_to_sibling(m, j)

    def q_step(m, partners):
        if m:
            await_recv(q_piece(m), qz_r.at[m - 1])
        to_z(q_piece, m, q_s, qz_r, partners)
        for j in range(1, NY):
            remote(q_piece(m), q_piece(m), q_s, qy_r, me.at(y=plus(y, j, NY))).start()

    await_recv(halves.at[other], ce_r.at[0])
    own_shard = w_piece(0)
    both = jnp.concatenate([halves[0], halves[1]], axis=0).astype(jnp.float32)
    both = jnp.concatenate([both, jnp.zeros((128, 96), jnp.float32)], axis=1)
    pair_rows[...] = both.T[:288].astype(jnp.bfloat16)
    own_shard[...] = pair_rows[pl.ds(pl.multiple_of(c * 144, 16), 144), :]
    w_step(0, (4, 2, 1))
    to_x(own_proj, proj_s, px_r)

    @pl.when(h == 1)
    def _():
        meet_other_half()
        remote(own_proj, own_proj, proj_s, pz_r, flip).start()


    await_recv(tokens.at[other], ce_r.at[1])
    mine = [
        jnp.where(c == 0, both[:, 0, :], both[:, 1, :]) for both in (tokens[i].astype(jnp.float32) for i in range(2))
    ]
    chip_tokens = jnp.concatenate(mine + [jnp.zeros((SLOT_ROWS - CHIP_ROWS, 1024), jnp.float32)], axis=0)

    def image(slot, first=0, count=SLOT_ROWS):
        return grid_img.at[pl.ds(pl.multiple_of(slot * SLOT_ROWS + first, 16), count)]

    image(my_slot, 0, BODY_ROWS)[...] = chip_tokens[:BODY_ROWS].astype(jnp.bfloat16)
    own_rest = chip_tokens[BODY_ROWS:CHIP_ROWS]
    rests[my_slot] = jnp.concatenate([own_rest[:, :512], own_rest[:, 512:]], axis=0).astype(jnp.bfloat16)
    to_x(image(my_slot, 0, BODY_ROWS), img_s, gx_r.at[0])
    to_x(rests.at[my_slot], rest_s, rx_r.at[0])

    def flip_cut(i):
        piece = image(my_slot, *CUTS[i])
        remote(piece, piece, img_s, gz_r.at[i], flip).start()

    def flip_rest():
        remote(rests.at[my_slot], rests.at[my_slot], rest_s, rz_r, flip).start()

    def image_step(i):
        piece = image(flip_slot, *CUTS[i])
        await_recv(piece, gz_r.at[i])
        to_x(piece, img_s, gx_r.at[1])

    def rest_step():
        await_recv(rests.at[flip_slot], rz_r)
        to_x(rests.at[flip_slot], rest_s, rx_r.at[1])

    def image_wait(which):
        await_recv(grid_img.at[pl.ds(0, (NX - 1) * BODY_ROWS)], gx_r.at[which])
        await_recv(rests.at[pl.ds(0, NX - 1)], rx_r.at[which])

    def put_rests(half):
        for i in range(NX):
            rest = rests[half * NX + i].astype(jnp.float32)
            rest = jnp.concatenate([rest[:8], rest[8:]], axis=1)
            rest = jnp.concatenate([rest, jnp.zeros((8, 1024), jnp.float32)], axis=0)
            image(half * NX + i, BODY_ROWS, 16)[...] = rest.astype(jnp.bfloat16)

    def multiply(half):
        put_rests(half)
        rows = pl.ds(pl.multiple_of(half * (NX * SLOT_ROWS), 64), NX * SLOT_ROWS)

        @pl.loop(0, 5)
        def _(n):
            rhs = jnp.concatenate(
                [
                    weights[pl.ds(pl.multiple_of(n * 2048, 1024), 1024), :],
                    weights[pl.ds(pl.multiple_of(n * 2048 + 1024, 1024), 1024), :],
                ],
                axis=1,
            )
            prod = jnp.dot(grid_img[rows, :], rhs, preferred_element_type=jnp.float32)
            z_ref[2 * n, rows, :] = prod[:, :128]
            z_ref[2 * n + 1, rows, :] = prod[:, 128:]

    row = lax.broadcasted_iota(jnp.int32, (1024, 128), 0)
    lane = lax.broadcasted_iota(jnp.int32, (1024, 128), 1)
    first = tb_ref[2 * my_slot] * 64
    second = tb_ref[2 * my_slot + 1] * 64 - 64
    wanted = lane + jnp.where(lane < 64, first, second)
    weights[pl.ds(9 * 1024, 1024), :] = jnp.where(row == wanted, 1.0, 0.0).astype(jnp.bfloat16)
    w_step(4, (2, 1))
    @pl.when(h == 1)
    def _():
        flip_cut(0)

    @pl.when(h == 0)
    def _():
        meet_other_half()
        remote(own_proj, own_proj, proj_s, pz_r, flip).start()
        flip_cut(0)
        flip_cut(1)
        flip_rest()

    w_step(2, (1,))
    w_step(6, (1,))
    @pl.when(h == 1)
    def _():
        flip_cut(1)
        flip_rest()

    await_recv(flip_proj, pz_r)
    to_x(flip_proj, proj_s, px_r)
    w_step(1, ())
    w_step(5, ())
    await_recv(proj_all.at[c, pl.ds(0, 2 * (NX - 1))], px_r)
    remote(proj_all.at[c], proj_all.at[c], proj_cs, pd_r, sibling).start()
    w_step(3, ())
    w_step(7, ())
    await_recv(proj_all.at[other], pd_r)
    holder = jnp.int32(0)
    for t in range(4 * NX):
        holder = jnp.where(tb_ref[t] == me.t, t, holder)
    q_piece(0)[...] = proj_all[lax.rem(holder, 2), holder // 2]
    q_step(0, (4, 2, 1))

    image_step(0)
    for j in range(1, NY):
        w_rest(j, 0)
    image_step(1)
    rest_step()
    for j in range(1, NY):
        w_rest(j, 1)
    @pl.when(h == 0)
    def _():
        q_step(4, (2, 1))

    await_recv(weights.at[pl.ds(0, NY * NZ * 144)], wd_r)
    image_wait(0)
    multiply(h)
    @pl.when(h == 0)
    def _():
        q_step(2, (1,))
        q_step(6, (1,))

    @pl.when(h == 1)
    def _():
        q_step(4, (2, 1))

    image_wait(1)
    multiply(1 - h)

    column = lax.broadcasted_iota(jnp.int32, (GRID, 128), 0)

    def product(tap, gy):
        return z_ref[tap, pl.ds((gy // 3) * SLOT_ROWS + (gy % 3) * GRID, GRID), :]

    for gy in range(0, GRID, 2):
        total = jnp.zeros((GRID, 128), jnp.float32)
        for row_y in (gy, gy + 1):
            parts = []
            for kx in range(3):
                part = None
                for ky in range(3):
                    if 0 <= row_y + ky - 1 < GRID:
                        value = product(3 * ky + kx, row_y + ky - 1)
                        part = value if part is None else part + value
                parts.append(part)
            left = jnp.where(column == 0, 0.0, pltpu.roll(parts[0], 1, 0))
            right = jnp.where(column == GRID - 1, 0.0, pltpu.roll(parts[2], GRID - 1, 0))
            value = parts[1] + left + right
            total = total + product(9, row_y) + value / (1.0 + jnp.exp(-value))
        fs_ref[pl.ds((gy // 2) * GRID, GRID), :] = total
    mean = (fs_ref[pl.ds(0, 144, stride=2), :] + fs_ref[pl.ds(1, 144, stride=2), :]) * 0.25
    own_pool[...] = mean.astype(jnp.bfloat16)

    def pool_to_x(piece, dst):
        for k in range(1, NX):
            remote(piece, dst, pool_s, ox_r, me.at(x=plus(x, k, NX), c=1)).start()

    remote(own_pool, pooled.at[c, my_slot], pool_s, oz_r.at[c], me.at(h=1 - h, c=1)).start()
    pool_to_x(own_pool, pooled.at[c, my_slot])

    @pl.when(c == 0)
    def _():
        remote(own_pool, pooled.at[0, my_slot], pool_cs, oc_r, sibling).start()

    @pl.when(c == 1)
    def _():
        pooled[1, my_slot] = own_pool[...]

    @pl.when(h == 1)
    def _():
        q_step(2, (1,))
        q_step(6, (1,))

    for m in (1, 5, 3, 7):
        q_step(m, ())
    @pl.when(c == 1)
    def _():
        for i in (1, 0):
            flip_pool = pooled.at[i, flip_slot]
            await_recv(flip_pool, oz_r.at[i])
            pool_to_x(flip_pool, flip_pool)

    await_recv(proj_cols.at[pl.ds(0, (NY - 1) * NZ)], qy_r)

    for t in range(4 * NX):
        block = tb_ref[t]
        proj_perm[pl.ds(t * 64, 32), :] = proj_cols[2 * block]
        proj_perm[pl.ds(t * 64 + 32, 32), :] = proj_cols[2 * block + 1]

    @pl.when(c == 1)
    def _():
        await_recv(pooled.at[0, my_slot], oc_r)
        await_recv(pooled.at[:, pl.ds(0, 2 * (NX - 1))], ox_r)
        remote(pooled, pooled, pool_cs, od_r, sibling).start()

    @pl.when(c == 0)
    def _():
        await_recv(pooled, od_r)

    def project(img):
        lhs = jnp.concatenate([pooled[img, s] for s in range(SLOTS)], axis=1)
        return jnp.dot(lhs, proj_perm[...], preferred_element_type=jnp.float32).astype(jnp.bfloat16)

    results = []
    for slot in range(2):
        result[slot] = project(slot_ref[slot])
        results.append(pltpu.make_async_copy(result.at[slot], out_ref.at[slot], loc.at[slot]))
        results[-1].start()

    ce_conv.wait_send()
    ce_img.wait_send()
    await_send(weights.at[pl.ds(0, (NZ - 1 + (NY - 1) * NZ + NY * NZ) * 144)], w_s)
    await_send(grid_img.at[pl.ds(0, (2 * (NX - 1) + 1) * BODY_ROWS)], img_s)
    await_send(rests.at[pl.ds(0, 2 * (NX - 1) + 1)], rest_s)
    await_send(proj_all.at[c, pl.ds(0, 2 * (NX - 1) + 1)], proj_s)
    await_send(proj_all.at[c], proj_cs)
    await_send(proj_cols.at[pl.ds(0, NZ - 1 + (NY - 1) * NZ)], q_s)
    @pl.when(c == 0)
    def _():
        await_send(pooled.at[0, pl.ds(0, NX)], pool_s)
        await_send(own_pool, pool_cs)

    @pl.when(c == 1)
    def _():
        await_send(pooled.at[:, pl.ds(0, (3 * (NX - 1) + 1) // 2)], pool_s)
        await_send(pooled, pool_cs)

    for copy in results:
        copy.wait()


def per_device(patches, image_slot, trainer_blocks, conv_weight, proj_weight):
    dma = pltpu.SemaphoreType.DMA
    anywhere = pl.BlockSpec(memory_space=pl.ANY)
    bf16, f32 = jnp.bfloat16, jnp.float32
    sems = [
        dma((2,)),
        dma,
        dma,
        dma,
        dma,
        dma,
        dma,
        dma,
        dma,
        dma((2,)),
        dma((NZ - 1,)),
        dma((2 * (NY - 1),)),
        dma,
        dma((len(CUTS),)),
        dma((2,)),
        dma,
        dma((2,)),
        dma,
        dma,
        dma,
        dma((NZ - 1,)),
        dma,
        dma((2,)),
        dma,
        dma,
        dma,
    ]
    return pl.pallas_call(
        kernel,
        out_shape=jax.ShapeDtypeStruct((2, 144, 512), bf16),
        in_specs=[pl.BlockSpec(memory_space=pltpu.HBM)] * 5,
        out_specs=anywhere,
        scratch_shapes=[
            pltpu.SMEM((16,), jnp.int32),
            pltpu.SMEM((2,), jnp.int32),
            pltpu.VMEM((2, 36, 2, 1024), bf16),
            pltpu.VMEM((2, 64, 288), bf16),
            pltpu.VMEM((288, 128), bf16),
            pltpu.VMEM((SLOTS * SLOT_ROWS, 1024), bf16),
            pltpu.VMEM((SLOTS, 16, 512), bf16),
            pltpu.VMEM((10 * 1024, 128), bf16),
            pltpu.VMEM((10, SLOTS * SLOT_ROWS, 128), f32),
            pltpu.VMEM((288, 128), f32),
            pltpu.VMEM((2, SLOTS, 144, 128), bf16),
            pltpu.VMEM((2, SLOTS, 32, 512), bf16),
            pltpu.VMEM((NY * NZ, 32, 512), bf16),
            pltpu.VMEM((1024, 512), bf16),
            pltpu.VMEM((144, 128), bf16),
            pltpu.VMEM((2, 144, 512), bf16),
            pltpu.SemaphoreType.REGULAR,
            pltpu.SemaphoreType.REGULAR,
            dma((5,)),
        ]
        + sems,
        compiler_params=pltpu.CompilerParams(
            collective_id=0, has_side_effects=True, vmem_limit_bytes=40 * 1024 * 1024
        ),
        cost_estimate=pl.CostEstimate(flops=2_000_000_000, bytes_accessed=600_000, transcendentals=73728),
        name="vision",
    )(*(pltpu.with_memory_space_constraint(a, pltpu.HBM) for a in (trainer_blocks, image_slot, jnp.transpose(patches, (1, 0, 2)), conv_weight.T, proj_weight)))


def solution(mesh):
    placed = (P("dp", "tp", None), P("dp"), P(), P("dp", "tp"), P("dp", "tp"))
    return jax.shard_map(
        per_device, mesh=mesh, in_specs=placed, out_specs=P("dp", None, "tp"), check_vma=False
    )
```

```python
import functools

import jax
import jax.numpy as jnp
from jax import lax
from jax.experimental import pallas as pl
from jax.experimental.pallas import tpu as pltpu
from jax.sharding import PartitionSpec as P

MESH = pl.DeviceIdType.MESH

GRID = 24
NX, NY, NZ = 4, 4, 8
SLOTS = 2 * NX
SLOT_ROWS = 80
CHIP_ROWS = 72
BODY_ROWS = 64
CUTS = ((0, 32), (32, 32))


class Place:
    def __init__(self):
        d = lax.axis_index("dp")
        t = lax.axis_index("tp")
        self.y, self.z = d // NZ, lax.rem(d, NZ)
        self.h, self.x, self.c = t // (2 * NX), lax.rem(t // 2, NX), lax.rem(t, 2)
        self.d, self.t = d, t
        self.slot = self.h * NX + self.x

    def at(self, y=None, z=None, h=None, x=None, c=None):
        y = self.y if y is None else y
        z = self.z if z is None else z
        h = self.h if h is None else h
        x = self.x if x is None else x
        c = self.c if c is None else c
        return (y * NZ + z, h * (2 * NX) + x * 2 + c)

    def sibling(self):
        return self.at(c=1 - self.c)

    def flip(self):
        return self.at(h=1 - self.h)


def plus(value, step, size):
    return lax.rem(value + step, size)


def kernel(
    tb_in,
    slot_in,
    patches,
    conv,
    proj,
    out_ref,
    tb_ref,
    slot_ref,
    tokens,
    halves,
    pair_rows,
    grid_img,
    rests,
    weights,
    z_ref,
    fs_ref,
    pooled,
    proj_all,
    proj_cols,
    proj_perm,
    own_pool,
    by_image,
    result,
    half_ok,
    flip_ok,
    loc,
    ce_s,
    w_s,
    img_s,
    rest_s,
    proj_s,
    proj_cs,
    q_s,
    pool_s,
    pool_cs,
    ce_r,
    wz_r,
    wy_r,
    wd_r,
    gz_r,
    gx_r,
    rz_r,
    rx_r,
    pz_r,
    px_r,
    pd_r,
    qz_r,
    qy_r,
    oz_r,
    ox_r,
    oc_r,
    od_r,
):
    me = Place()
    c, h, x, y, z, d = me.c, me.h, me.x, me.y, me.z, me.d
    other = 1 - c
    sibling, flip = me.sibling(), me.flip()
    my_slot = me.slot
    flip_slot = (1 - h) * NX + x

    def remote(src, dst, send, recv, where):
        return pltpu.make_async_remote_copy(
            src_ref=src, dst_ref=dst, send_sem=send, recv_sem=recv, device_id=where, device_id_type=MESH
        )

    def await_recv(dst, recv):
        remote(dst, dst, recv, recv, sibling).wait_recv()

    def await_send(src, send):
        remote(src, src, send, send, sibling).wait_send()

    bits = (lax.rem(z, 2), lax.rem(z // 2, 2), z // 4)

    def across(m):
        return sum((1 - bit if m >> i & 1 else bit) * (1 << i) for i, bit in enumerate(bits))

    barrier = pltpu.get_barrier_semaphore()

    def greet(where):
        pl.semaphore_signal(barrier, inc=1, device_id=where, device_id_type=MESH)

    for k in range(1, NZ):
        greet(me.at(z=plus(z, k, NZ), c=1))
    for k in range(1, NX):
        greet(me.at(x=plus(x, k, NX), c=1))
    for k in range(1, NY):
        greet(me.at(y=plus(y, k, NY), c=1))

    @pl.when(c == 0)
    def _():
        greet(sibling)

    greet(me.at(h=1 - h, c=0))

    local = [
        pltpu.make_async_copy(patches, tokens.at[c], loc.at[0]),
        pltpu.make_async_copy(conv, halves.at[c], loc.at[1]),
        pltpu.make_async_copy(proj, proj_all.at[c, my_slot], loc.at[2]),
        pltpu.make_async_copy(tb_in, tb_ref, loc.at[3]),
        pltpu.make_async_copy(slot_in, slot_ref, loc.at[4]),
    ]
    for copy in local:
        copy.start()

    for copy in local:
        copy.wait()
    @pl.when(c == 1)
    def _():
        pl.semaphore_wait(barrier, 2 * (NZ - 1 + NX - 1 + NY - 1) + 1)
        pl.semaphore_signal(half_ok, inc=1, device_id=sibling, device_id_type=MESH)

    @pl.when(c == 0)
    def _():
        pl.semaphore_wait(half_ok, 1)

    def meet_other_half():
        @pl.when(c == 0)
        def _():
            pl.semaphore_wait(barrier, 2)
            pl.semaphore_signal(flip_ok, inc=1, device_id=sibling, device_id_type=MESH)

        @pl.when(c == 1)
        def _():
            pl.semaphore_wait(flip_ok, 1)


    ce_conv = remote(halves.at[c], halves.at[c], ce_s.at[0], ce_r.at[0], sibling)
    ce_conv.start()
    ce_img = remote(tokens.at[c], tokens.at[c], ce_s.at[1], ce_r.at[1], sibling)
    ce_img.start()
    own_proj = proj_all.at[c, my_slot]
    flip_proj = proj_all.at[c, flip_slot]

    def to_x(piece, send, recv):
        for k in range(1, NX):
            remote(piece, piece, send, recv, me.at(x=plus(x, k, NX))).start()

    def shard(dp, core):
        return weights.at[pl.ds(pl.multiple_of(dp * 288 + core * 144, 16), 144)]

    def w_piece(m, j=0):
        return shard(plus(y, NY - j, NY) * NZ + across(m), c)

    def q_piece(m, j=0):
        return proj_cols.at[plus(y, NY - j, NY) * NZ + across(m)]

    def to_z(piece, m, send, recvs, partners):
        for p in partners:
            remote(piece(m), piece(m), send, recvs.at[(m ^ p) - 1], me.at(z=across(p))).start()

    def w_to_sibling(m, j):
        remote(w_piece(m, j), w_piece(m, j), w_s, wd_r, sibling).start()

    def w_step(m, partners):
        if m:
            await_recv(w_piece(m), wz_r.at[m - 1])
        to_z(w_piece, m, w_s, wz_r, partners)
        for j in range(1, NY):
            remote(w_piece(m), w_piece(m), w_s, wy_r.at[2 * (j - 1) + m % 2], me.at(y=plus(y, j, NY))).start()
        w_to_sibling(m, 0)

    def w_rest(j, odd):
        await_recv(weights.at[pl.ds(0, 4 * 144)], wy_r.at[2 * (j - 1) + odd])
        for m in range(odd, NZ, 2):
            w_to_sibling(m, j)

    def q_step(m, partners):
        if m:
            await_recv(q_piece(m), qz_r.at[m - 1])
        to_z(q_piece, m, q_s, qz_r, partners)
        for j in range(1, NY):
            remote(q_piece(m), q_piece(m), q_s, qy_r, me.at(y=plus(y, j, NY))).start()

    def proj_along_x():
        await_recv(flip_proj, pz_r)
        to_x(flip_proj, proj_s, px_r)

    def proj_to_sibling():
        await_recv(proj_all.at[c, pl.ds(0, 2 * (NX - 1))], px_r)
        remote(proj_all.at[c], proj_all.at[c], proj_cs, pd_r, sibling).start()

    def proj_select():
        await_recv(proj_all.at[other], pd_r)
        holder = jnp.int32(0)
        for t in range(4 * NX):
            holder = jnp.where(tb_ref[t] == me.t, t, holder)
        q_piece(0)[...] = proj_all[lax.rem(holder, 2), holder // 2]
        q_step(0, (4, 2, 1))

    await_recv(halves.at[other], ce_r.at[0])
    own_shard = w_piece(0)
    both = jnp.concatenate([halves[0], halves[1]], axis=0).astype(jnp.float32)
    both = jnp.concatenate([both, jnp.zeros((128, 96), jnp.float32)], axis=1)
    pair_rows[...] = both.T[:288].astype(jnp.bfloat16)
    own_shard[...] = pair_rows[pl.ds(pl.multiple_of(c * 144, 16), 144), :]
    w_step(0, (4, 2, 1))
    to_x(own_proj, proj_s, px_r)

    @pl.when(h == 1)
    def _():
        meet_other_half()
        remote(own_proj, own_proj, proj_s, pz_r, flip).start()


    await_recv(tokens.at[other], ce_r.at[1])
    mine = [
        jnp.where(c == 0, both[:, 0, :], both[:, 1, :]) for both in (tokens[i].astype(jnp.float32) for i in range(2))
    ]
    chip_tokens = jnp.concatenate(mine + [jnp.zeros((SLOT_ROWS - CHIP_ROWS, 1024), jnp.float32)], axis=0)

    def image(slot, first=0, count=SLOT_ROWS):
        return grid_img.at[pl.ds(pl.multiple_of(slot * SLOT_ROWS + first, 16), count)]

    image(my_slot, 0, BODY_ROWS)[...] = chip_tokens[:BODY_ROWS].astype(jnp.bfloat16)
    own_rest = chip_tokens[BODY_ROWS:CHIP_ROWS]
    rests[my_slot] = jnp.concatenate([own_rest[:, :512], own_rest[:, 512:]], axis=0).astype(jnp.bfloat16)
    to_x(image(my_slot, 0, BODY_ROWS), img_s, gx_r.at[0])
    to_x(rests.at[my_slot], rest_s, rx_r.at[0])

    def flip_cut(i):
        piece = image(my_slot, *CUTS[i])
        remote(piece, piece, img_s, gz_r.at[i], flip).start()

    def flip_rest():
        remote(rests.at[my_slot], rests.at[my_slot], rest_s, rz_r, flip).start()

    def image_step(i):
        piece = image(flip_slot, *CUTS[i])
        await_recv(piece, gz_r.at[i])
        to_x(piece, img_s, gx_r.at[1])

    def rest_step():
        await_recv(rests.at[flip_slot], rz_r)
        to_x(rests.at[flip_slot], rest_s, rx_r.at[1])

    def image_wait(which):
        await_recv(grid_img.at[pl.ds(0, (NX - 1) * BODY_ROWS)], gx_r.at[which])
        await_recv(rests.at[pl.ds(0, NX - 1)], rx_r.at[which])

    def put_rests(half):
        for i in range(NX):
            rest = rests[half * NX + i].astype(jnp.float32)
            rest = jnp.concatenate([rest[:8], rest[8:]], axis=1)
            rest = jnp.concatenate([rest, jnp.zeros((8, 1024), jnp.float32)], axis=0)
            image(half * NX + i, BODY_ROWS, 16)[...] = rest.astype(jnp.bfloat16)

    def multiply(half):
        put_rests(half)
        rows = pl.ds(pl.multiple_of(half * (NX * SLOT_ROWS), 64), NX * SLOT_ROWS)

        @pl.loop(0, 5)
        def _(n):
            rhs = jnp.concatenate(
                [
                    weights[pl.ds(pl.multiple_of(n * 2048, 1024), 1024), :],
                    weights[pl.ds(pl.multiple_of(n * 2048 + 1024, 1024), 1024), :],
                ],
                axis=1,
            )
            prod = jnp.dot(grid_img[rows, :], rhs, preferred_element_type=jnp.float32)
            z_ref[2 * n, rows, :] = prod[:, :128]
            z_ref[2 * n + 1, rows, :] = prod[:, 128:]

    @pl.when(h == 0)
    def _():
        meet_other_half()
        remote(own_proj, own_proj, proj_s, pz_r, flip).start()

    row = lax.broadcasted_iota(jnp.int32, (1024, 128), 0)
    lane = lax.broadcasted_iota(jnp.int32, (1024, 128), 1)
    first = tb_ref[2 * my_slot] * 64
    second = tb_ref[2 * my_slot + 1] * 64 - 64
    wanted = lane + jnp.where(lane < 64, first, second)
    weights[pl.ds(9 * 1024, 1024), :] = jnp.where(row == wanted, 1.0, 0.0).astype(jnp.bfloat16)
    w_step(4, (2, 1))
    @pl.when(h == 1)
    def _():
        flip_cut(0)

    @pl.when(h == 0)
    def _():
        flip_cut(0)
        flip_cut(1)
        flip_rest()

    w_step(2, (1,))
    w_step(6, (1,))
    @pl.when(h == 1)
    def _():
        flip_cut(1)
        flip_rest()

    proj_along_x()
    w_step(1, ())
    w_step(5, ())
    proj_to_sibling()
    w_step(3, ())
    w_step(7, ())
    proj_select()

    image_step(0)
    for j in range(1, NY):
        w_rest(j, 0)
    image_step(1)
    rest_step()
    for j in range(1, NY):
        w_rest(j, 1)
    @pl.when(h == 0)
    def _():
        q_step(4, (2, 1))

    await_recv(weights.at[pl.ds(0, NY * NZ * 144)], wd_r)
    image_wait(0)
    multiply(h)
    @pl.when(h == 0)
    def _():
        q_step(2, (1,))
        q_step(6, (1,))

    @pl.when(h == 1)
    def _():
        q_step(4, (2, 1))

    image_wait(1)
    multiply(1 - h)

    column = lax.broadcasted_iota(jnp.int32, (GRID, 128), 0)

    def product(tap, gy):
        return z_ref[tap, pl.ds((gy // 3) * SLOT_ROWS + (gy % 3) * GRID, GRID), :]

    for gy in range(0, GRID, 2):
        total = jnp.zeros((GRID, 128), jnp.float32)
        for row_y in (gy, gy + 1):
            parts = []
            for kx in range(3):
                part = None
                for ky in range(3):
                    if 0 <= row_y + ky - 1 < GRID:
                        value = product(3 * ky + kx, row_y + ky - 1)
                        part = value if part is None else part + value
                parts.append(part)
            left = jnp.where(column == 0, 0.0, pltpu.roll(parts[0], 1, 0))
            right = jnp.where(column == GRID - 1, 0.0, pltpu.roll(parts[2], GRID - 1, 0))
            value = parts[1] + left + right
            total = total + product(9, row_y) + value / (1.0 + jnp.exp(-value))
        fs_ref[pl.ds((gy // 2) * GRID, GRID), :] = total
    mean = (fs_ref[pl.ds(0, 144, stride=2), :] + fs_ref[pl.ds(1, 144, stride=2), :]) * 0.25
    own_pool[...] = mean.astype(jnp.bfloat16)

    def pool_to_x(piece, dst, half):
        for k in range(1, NX):
            remote(piece, dst, pool_s, ox_r.at[half], me.at(x=plus(x, k, NX), c=1)).start()

    remote(own_pool, pooled.at[c, my_slot], pool_s, oz_r.at[c], me.at(h=1 - h, c=1)).start()
    pool_to_x(own_pool, pooled.at[c, my_slot], 0)

    @pl.when(c == 0)
    def _():
        remote(own_pool, pooled.at[0, my_slot], pool_cs, oc_r, sibling).start()

    @pl.when(c == 1)
    def _():
        pooled[1, my_slot] = own_pool[...]

    @pl.when(h == 1)
    def _():
        q_step(2, (1,))
        q_step(6, (1,))

    for m in (1, 5, 3, 7):
        q_step(m, ())
    @pl.when(c == 1)
    def _():
        for i in (1, 0):
            flip_pool = pooled.at[i, flip_slot]
            await_recv(flip_pool, oz_r.at[i])
            pool_to_x(flip_pool, flip_pool, 1)

    def pool_of_half(half):
        return pooled.at[:, pl.ds((h if half == 0 else 1 - h) * NX, NX)]

    def pool_to_first(half):
        await_recv(pooled.at[:, pl.ds(0, NX - 1)], ox_r.at[half])
        remote(pool_of_half(half), pool_of_half(half), pool_cs, od_r.at[half], sibling).start()

    @pl.when(c == 1)
    def _():
        await_recv(pooled.at[0, my_slot], oc_r)
        pool_to_first(0)

    await_recv(proj_cols.at[pl.ds(0, (NY - 1) * NZ)], qy_r)

    for t in range(4 * NX):
        block = tb_ref[t]
        proj_perm[pl.ds(t * 64, 32), :] = proj_cols[2 * block]
        proj_perm[pl.ds(t * 64 + 32, 32), :] = proj_cols[2 * block + 1]

    @pl.when(c == 0)
    def _():
        await_recv(pool_of_half(0), od_r.at[0])

    def project(half):
        first = (h if half == 0 else 1 - h) * NX
        rows = pl.ds(pl.multiple_of(first * 128, 512), 512)
        lhs = jnp.concatenate(
            [jnp.concatenate([pooled[i, first + s] for s in range(NX)], axis=1) for i in range(2)], axis=0
        )
        return jnp.dot(lhs, proj_perm[rows, :], preferred_element_type=jnp.float32)

    half_sum = project(0)
    for i in range(2):
        by_image[i] = half_sum[144 * i : 144 * (i + 1)]
    @pl.when(c == 1)
    def _():
        pool_to_first(1)

    @pl.when(c == 0)
    def _():
        await_recv(pool_of_half(1), od_r.at[1])

    half_sum = project(1)
    for i in range(2):
        by_image[i] += half_sum[144 * i : 144 * (i + 1)]
    results = []
    for slot in range(2):
        result[slot] = by_image[slot_ref[slot]].astype(jnp.bfloat16)
        results.append(pltpu.make_async_copy(result.at[slot], out_ref.at[slot], loc.at[slot]))
        results[-1].start()

    ce_conv.wait_send()
    ce_img.wait_send()
    await_send(weights.at[pl.ds(0, (NZ - 1 + (NY - 1) * NZ + NY * NZ) * 144)], w_s)
    await_send(grid_img.at[pl.ds(0, (2 * (NX - 1) + 1) * BODY_ROWS)], img_s)
    await_send(rests.at[pl.ds(0, 2 * (NX - 1) + 1)], rest_s)
    await_send(proj_all.at[c, pl.ds(0, 2 * (NX - 1) + 1)], proj_s)
    await_send(proj_all.at[c], proj_cs)
    await_send(proj_cols.at[pl.ds(0, NZ - 1 + (NY - 1) * NZ)], q_s)
    @pl.when(c == 0)
    def _():
        await_send(pooled.at[0, pl.ds(0, NX)], pool_s)
        await_send(own_pool, pool_cs)

    @pl.when(c == 1)
    def _():
        await_send(pooled.at[:, pl.ds(0, (3 * (NX - 1) + 1) // 2)], pool_s)
        await_send(pooled, pool_cs)

    for copy in results:
        copy.wait()


def per_device(patches, image_slot, trainer_blocks, conv_weight, proj_weight):
    dma = pltpu.SemaphoreType.DMA
    anywhere = pl.BlockSpec(memory_space=pl.ANY)
    bf16, f32 = jnp.bfloat16, jnp.float32
    sems = [
        dma((2,)),
        dma,
        dma,
        dma,
        dma,
        dma,
        dma,
        dma,
        dma,
        dma((2,)),
        dma((NZ - 1,)),
        dma((2 * (NY - 1),)),
        dma,
        dma((len(CUTS),)),
        dma((2,)),
        dma,
        dma((2,)),
        dma,
        dma,
        dma,
        dma((NZ - 1,)),
        dma,
        dma((2,)),
        dma((2,)),
        dma,
        dma((2,)),
    ]
    return pl.pallas_call(
        kernel,
        out_shape=jax.ShapeDtypeStruct((2, 144, 512), bf16),
        in_specs=[pl.BlockSpec(memory_space=pltpu.HBM)] * 5,
        out_specs=anywhere,
        scratch_shapes=[
            pltpu.SMEM((16,), jnp.int32),
            pltpu.SMEM((2,), jnp.int32),
            pltpu.VMEM((2, 36, 2, 1024), bf16),
            pltpu.VMEM((2, 64, 288), bf16),
            pltpu.VMEM((288, 128), bf16),
            pltpu.VMEM((SLOTS * SLOT_ROWS, 1024), bf16),
            pltpu.VMEM((SLOTS, 16, 512), bf16),
            pltpu.VMEM((10 * 1024, 128), bf16),
            pltpu.VMEM((10, SLOTS * SLOT_ROWS, 128), f32),
            pltpu.VMEM((288, 128), f32),
            pltpu.VMEM((2, SLOTS, 144, 128), bf16),
            pltpu.VMEM((2, SLOTS, 32, 512), bf16),
            pltpu.VMEM((NY * NZ, 32, 512), bf16),
            pltpu.VMEM((1024, 512), bf16),
            pltpu.VMEM((144, 128), bf16),
            pltpu.VMEM((2, 144, 512), f32),
            pltpu.VMEM((2, 144, 512), bf16),
            pltpu.SemaphoreType.REGULAR,
            pltpu.SemaphoreType.REGULAR,
            dma((5,)),
        ]
        + sems,
        compiler_params=pltpu.CompilerParams(
            collective_id=0, has_side_effects=True, vmem_limit_bytes=40 * 1024 * 1024
        ),
        cost_estimate=pl.CostEstimate(flops=2_000_000_000, bytes_accessed=600_000, transcendentals=73728),
        name="vision",
    )(*(pltpu.with_memory_space_constraint(a, pltpu.HBM) for a in (trainer_blocks, image_slot, jnp.transpose(patches, (1, 0, 2)), conv_weight.T, proj_weight)))


def solution(mesh):
    placed = (P("dp", "tp", None), P("dp"), P(), P("dp", "tp"), P("dp", "tp"))
    return jax.shard_map(
        per_device, mesh=mesh, in_specs=placed, out_specs=P("dp", None, "tp"), check_vma=False
    )
```

```python
import functools

import jax
import jax.numpy as jnp
from jax import lax
from jax.experimental import pallas as pl
from jax.experimental.pallas import tpu as pltpu
from jax.sharding import PartitionSpec as P

MESH = pl.DeviceIdType.MESH

GRID = 24
NX, NY, NZ = 4, 4, 8
SLOTS = 2 * NX
SLOT_ROWS = 80
CHIP_ROWS = 72
BODY_ROWS = 64
CUTS = ((0, 32), (32, 32))


class Place:
    def __init__(self):
        d = lax.axis_index("dp")
        t = lax.axis_index("tp")
        self.y, self.z = d // NZ, lax.rem(d, NZ)
        self.h, self.x, self.c = t // (2 * NX), lax.rem(t // 2, NX), lax.rem(t, 2)
        self.d, self.t = d, t
        self.slot = self.h * NX + self.x

    def at(self, y=None, z=None, h=None, x=None, c=None):
        y = self.y if y is None else y
        z = self.z if z is None else z
        h = self.h if h is None else h
        x = self.x if x is None else x
        c = self.c if c is None else c
        return (y * NZ + z, h * (2 * NX) + x * 2 + c)

    def sibling(self):
        return self.at(c=1 - self.c)

    def flip(self):
        return self.at(h=1 - self.h)


def plus(value, step, size):
    return lax.rem(value + step, size)


def kernel(
    tb_in,
    slot_in,
    patches,
    conv,
    proj,
    out_ref,
    tb_ref,
    slot_ref,
    tokens,
    halves,
    pair_rows,
    grid_img,
    rests,
    weights,
    z_ref,
    fs_ref,
    pooled,
    proj_all,
    proj_cols,
    proj_perm,
    own_pool,
    by_image,
    result,
    half_ok,
    flip_ok,
    loc,
    ce_s,
    w_s,
    img_s,
    rest_s,
    proj_s,
    proj_cs,
    q_s,
    pool_s,
    pool_cs,
    ce_r,
    wz_r,
    wy_r,
    wd_r,
    gz_r,
    gx_r,
    rz_r,
    rx_r,
    pz_r,
    px_r,
    pd_r,
    qz_r,
    qy_r,
    oz_r,
    ox_r,
    oc_r,
    od_r,
):
    me = Place()
    c, h, x, y, z, d = me.c, me.h, me.x, me.y, me.z, me.d
    other = 1 - c
    sibling, flip = me.sibling(), me.flip()
    my_slot = me.slot
    flip_slot = (1 - h) * NX + x

    def remote(src, dst, send, recv, where):
        return pltpu.make_async_remote_copy(
            src_ref=src, dst_ref=dst, send_sem=send, recv_sem=recv, device_id=where, device_id_type=MESH
        )

    def await_recv(dst, recv):
        remote(dst, dst, recv, recv, sibling).wait_recv()

    def await_send(src, send):
        remote(src, src, send, send, sibling).wait_send()

    bits = (lax.rem(z, 2), lax.rem(z // 2, 2), z // 4)

    def across(m):
        return sum((1 - bit if m >> i & 1 else bit) * (1 << i) for i, bit in enumerate(bits))

    barrier = pltpu.get_barrier_semaphore()

    def greet(where):
        pl.semaphore_signal(barrier, inc=1, device_id=where, device_id_type=MESH)

    for k in range(1, NZ):
        greet(me.at(z=plus(z, k, NZ), c=1))
    for k in range(1, NX):
        greet(me.at(x=plus(x, k, NX), c=1))
    for k in range(1, NY):
        greet(me.at(y=plus(y, k, NY), c=1))

    @pl.when(c == 0)
    def _():
        greet(sibling)

    greet(me.at(h=1 - h, c=0))

    local = [
        pltpu.make_async_copy(patches, tokens.at[c], loc.at[0]),
        pltpu.make_async_copy(conv, halves.at[c], loc.at[1]),
        pltpu.make_async_copy(proj, proj_all.at[c, my_slot], loc.at[2]),
        pltpu.make_async_copy(tb_in, tb_ref, loc.at[3]),
        pltpu.make_async_copy(slot_in, slot_ref, loc.at[4]),
    ]
    for copy in local:
        copy.start()

    for copy in local:
        copy.wait()
    @pl.when(c == 1)
    def _():
        pl.semaphore_wait(barrier, 2 * (NZ - 1 + NX - 1 + NY - 1) + 1)
        pl.semaphore_signal(half_ok, inc=1, device_id=sibling, device_id_type=MESH)

    @pl.when(c == 0)
    def _():
        pl.semaphore_wait(half_ok, 1)

    def meet_other_half():
        @pl.when(c == 0)
        def _():
            pl.semaphore_wait(barrier, 2)
            pl.semaphore_signal(flip_ok, inc=1, device_id=sibling, device_id_type=MESH)

        @pl.when(c == 1)
        def _():
            pl.semaphore_wait(flip_ok, 1)


    ce_conv = remote(halves.at[c], halves.at[c], ce_s.at[0], ce_r.at[0], sibling)
    ce_conv.start()
    ce_img = remote(tokens.at[c], tokens.at[c], ce_s.at[1], ce_r.at[1], sibling)
    ce_img.start()
    own_proj = proj_all.at[c, my_slot]
    flip_proj = proj_all.at[c, flip_slot]

    def to_x(piece, send, recv):
        for k in range(1, NX):
            remote(piece, piece, send, recv, me.at(x=plus(x, k, NX))).start()

    def shard(dp, core):
        return weights.at[pl.ds(pl.multiple_of(dp * 288 + core * 144, 16), 144)]

    def w_piece(m, j=0):
        return shard(plus(y, NY - j, NY) * NZ + across(m), c)

    def q_piece(m, j=0):
        return proj_cols.at[plus(y, NY - j, NY) * NZ + across(m)]

    def to_z(piece, m, send, recvs, partners):
        for p in partners:
            remote(piece(m), piece(m), send, recvs.at[(m ^ p) - 1], me.at(z=across(p))).start()

    def w_to_sibling(m, j):
        remote(w_piece(m, j), w_piece(m, j), w_s, wd_r, sibling).start()

    def w_step(m, partners):
        if m:
            await_recv(w_piece(m), wz_r.at[m - 1])
        to_z(w_piece, m, w_s, wz_r, partners)
        for j in range(1, NY):
            remote(w_piece(m), w_piece(m), w_s, wy_r.at[2 * (j - 1) + m % 2], me.at(y=plus(y, j, NY))).start()
        w_to_sibling(m, 0)

    def w_rest(j, odd):
        await_recv(weights.at[pl.ds(0, 4 * 144)], wy_r.at[2 * (j - 1) + odd])
        for m in range(odd, NZ, 2):
            w_to_sibling(m, j)

    def q_step(m, partners):
        if m:
            await_recv(q_piece(m), qz_r.at[m - 1])
        to_z(q_piece, m, q_s, qz_r, partners)
        for j in range(1, NY):
            remote(q_piece(m), q_piece(m), q_s, qy_r, me.at(y=plus(y, j, NY))).start()

    def proj_along_x():
        await_recv(flip_proj, pz_r)
        to_x(flip_proj, proj_s, px_r)

    def proj_to_sibling():
        await_recv(proj_all.at[c, pl.ds(0, 2 * (NX - 1))], px_r)
        remote(proj_all.at[c], proj_all.at[c], proj_cs, pd_r, sibling).start()

    def proj_select():
        await_recv(proj_all.at[other], pd_r)
        holder = jnp.int32(0)
        for t in range(4 * NX):
            holder = jnp.where(tb_ref[t] == me.t, t, holder)
        q_piece(0)[...] = proj_all[lax.rem(holder, 2), holder // 2]

    await_recv(halves.at[other], ce_r.at[0])
    own_shard = w_piece(0)
    both = jnp.concatenate([halves[0], halves[1]], axis=0).astype(jnp.float32)
    both = jnp.concatenate([both, jnp.zeros((128, 96), jnp.float32)], axis=1)
    pair_rows[...] = both.T[:288].astype(jnp.bfloat16)
    own_shard[...] = pair_rows[pl.ds(pl.multiple_of(c * 144, 16), 144), :]
    w_step(0, (4, 2, 1))
    to_x(own_proj, proj_s, px_r)

    @pl.when(h == 1)
    def _():
        meet_other_half()
        remote(own_proj, own_proj, proj_s, pz_r, flip).start()


    await_recv(tokens.at[other], ce_r.at[1])
    mine = [
        jnp.where(c == 0, both[:, 0, :], both[:, 1, :]) for both in (tokens[i].astype(jnp.float32) for i in range(2))
    ]
    chip_tokens = jnp.concatenate(mine + [jnp.zeros((SLOT_ROWS - CHIP_ROWS, 1024), jnp.float32)], axis=0)

    def image(slot, first=0, count=SLOT_ROWS):
        return grid_img.at[pl.ds(pl.multiple_of(slot * SLOT_ROWS + first, 16), count)]

    image(my_slot, 0, BODY_ROWS)[...] = chip_tokens[:BODY_ROWS].astype(jnp.bfloat16)
    own_rest = chip_tokens[BODY_ROWS:CHIP_ROWS]
    rests[my_slot] = jnp.concatenate([own_rest[:, :512], own_rest[:, 512:]], axis=0).astype(jnp.bfloat16)
    to_x(image(my_slot, 0, BODY_ROWS), img_s, gx_r.at[0])
    to_x(rests.at[my_slot], rest_s, rx_r.at[0])

    def flip_cut(i):
        piece = image(my_slot, *CUTS[i])
        remote(piece, piece, img_s, gz_r.at[i], flip).start()

    def flip_rest():
        remote(rests.at[my_slot], rests.at[my_slot], rest_s, rz_r, flip).start()

    def image_step(i):
        piece = image(flip_slot, *CUTS[i])
        await_recv(piece, gz_r.at[i])
        to_x(piece, img_s, gx_r.at[1])

    def rest_step():
        await_recv(rests.at[flip_slot], rz_r)
        to_x(rests.at[flip_slot], rest_s, rx_r.at[1])

    def image_wait(which):
        await_recv(grid_img.at[pl.ds(0, (NX - 1) * BODY_ROWS)], gx_r.at[which])
        await_recv(rests.at[pl.ds(0, NX - 1)], rx_r.at[which])

    def put_rests(half):
        for i in range(NX):
            rest = rests[half * NX + i].astype(jnp.float32)
            rest = jnp.concatenate([rest[:8], rest[8:]], axis=1)
            rest = jnp.concatenate([rest, jnp.zeros((8, 1024), jnp.float32)], axis=0)
            image(half * NX + i, BODY_ROWS, 16)[...] = rest.astype(jnp.bfloat16)

    def multiply(half):
        put_rests(half)
        rows = pl.ds(pl.multiple_of(half * (NX * SLOT_ROWS), 64), NX * SLOT_ROWS)

        @pl.loop(0, 5)
        def _(n):
            rhs = jnp.concatenate(
                [
                    weights[pl.ds(pl.multiple_of(n * 2048, 1024), 1024), :],
                    weights[pl.ds(pl.multiple_of(n * 2048 + 1024, 1024), 1024), :],
                ],
                axis=1,
            )
            prod = jnp.dot(grid_img[rows, :], rhs, preferred_element_type=jnp.float32)
            z_ref[2 * n, rows, :] = prod[:, :128]
            z_ref[2 * n + 1, rows, :] = prod[:, 128:]

    @pl.when(h == 0)
    def _():
        meet_other_half()
        remote(own_proj, own_proj, proj_s, pz_r, flip).start()

    row = lax.broadcasted_iota(jnp.int32, (1024, 128), 0)
    lane = lax.broadcasted_iota(jnp.int32, (1024, 128), 1)
    first = tb_ref[2 * my_slot] * 64
    second = tb_ref[2 * my_slot + 1] * 64 - 64
    wanted = lane + jnp.where(lane < 64, first, second)
    weights[pl.ds(9 * 1024, 1024), :] = jnp.where(row == wanted, 1.0, 0.0).astype(jnp.bfloat16)
    w_step(4, (2, 1))
    @pl.when(h == 1)
    def _():
        flip_cut(0)

    @pl.when(h == 0)
    def _():
        flip_cut(0)
        flip_cut(1)
        flip_rest()

    w_step(2, (1,))
    w_step(6, (1,))
    @pl.when(h == 1)
    def _():
        flip_cut(1)
        flip_rest()

    proj_along_x()
    w_step(1, ())
    w_step(5, ())
    proj_to_sibling()
    @pl.when(h == 0)
    def _():
        proj_select()
        q_step(0, (4, 1, 2, 3))

    w_step(3, ())
    w_step(7, ())
    @pl.when(h == 1)
    def _():
        proj_select()
        q_step(0, (4, 2, 1))


    image_step(0)
    for j in range(1, NY):
        w_rest(j, 0)
    image_step(1)
    rest_step()
    @pl.when(h == 0)
    def _():
        q_step(4, (1, 2, 3))

    @pl.when(h == 0)
    def _():
        for m in (1, 2, 3):
            q_step(m, ())

    for j in range(1, NY):
        w_rest(j, 1)
    await_recv(weights.at[pl.ds(0, NY * NZ * 144)], wd_r)
    image_wait(0)
    multiply(h)
    image_wait(1)
    @pl.when(h == 0)
    def _():
        for m in (5, 6, 7):
            q_step(m, ())

    multiply(1 - h)

    column = lax.broadcasted_iota(jnp.int32, (GRID, 128), 0)

    def product(tap, gy):
        return z_ref[tap, pl.ds((gy // 3) * SLOT_ROWS + (gy % 3) * GRID, GRID), :]

    for gy in range(0, GRID, 2):
        total = jnp.zeros((GRID, 128), jnp.float32)
        for row_y in (gy, gy + 1):
            parts = []
            for kx in range(3):
                part = None
                for ky in range(3):
                    if 0 <= row_y + ky - 1 < GRID:
                        value = product(3 * ky + kx, row_y + ky - 1)
                        part = value if part is None else part + value
                parts.append(part)
            left = jnp.where(column == 0, 0.0, pltpu.roll(parts[0], 1, 0))
            right = jnp.where(column == GRID - 1, 0.0, pltpu.roll(parts[2], GRID - 1, 0))
            value = parts[1] + left + right
            total = total + product(9, row_y) + value / (1.0 + jnp.exp(-value))
        fs_ref[pl.ds((gy // 2) * GRID, GRID), :] = total
    mean = (fs_ref[pl.ds(0, 144, stride=2), :] + fs_ref[pl.ds(1, 144, stride=2), :]) * 0.25
    own_pool[...] = mean.astype(jnp.bfloat16)

    def pool_to_x(piece, dst, half):
        for k in range(1, NX):
            remote(piece, dst, pool_s, ox_r.at[half], me.at(x=plus(x, k, NX), c=1)).start()

    remote(own_pool, pooled.at[c, my_slot], pool_s, oz_r.at[c], me.at(h=1 - h, c=1)).start()
    pool_to_x(own_pool, pooled.at[c, my_slot], 0)

    @pl.when(c == 0)
    def _():
        remote(own_pool, pooled.at[0, my_slot], pool_cs, oc_r, sibling).start()

    @pl.when(c == 1)
    def _():
        pooled[1, my_slot] = own_pool[...]

    @pl.when(h == 1)
    def _():
        q_step(4, (2, 1))

    @pl.when(h == 1)
    def _():
        q_step(2, (1,))
        q_step(6, (1,))

    @pl.when(h == 1)
    def _():
        for m in (1, 5, 3, 7):
            q_step(m, ())

    @pl.when(c == 1)
    def _():
        for i in (1, 0):
            flip_pool = pooled.at[i, flip_slot]
            await_recv(flip_pool, oz_r.at[i])
            pool_to_x(flip_pool, flip_pool, 1)

    def pool_of_half(half):
        return pooled.at[:, pl.ds((h if half == 0 else 1 - h) * NX, NX)]

    def pool_to_first(half):
        await_recv(pooled.at[:, pl.ds(0, NX - 1)], ox_r.at[half])
        remote(pool_of_half(half), pool_of_half(half), pool_cs, od_r.at[half], sibling).start()

    @pl.when(c == 1)
    def _():
        await_recv(pooled.at[0, my_slot], oc_r)
        pool_to_first(0)

    await_recv(proj_cols.at[pl.ds(0, (NY - 1) * NZ)], qy_r)

    for t in range(4 * NX):
        block = tb_ref[t]
        proj_perm[pl.ds(t * 64, 32), :] = proj_cols[2 * block]
        proj_perm[pl.ds(t * 64 + 32, 32), :] = proj_cols[2 * block + 1]

    @pl.when(c == 0)
    def _():
        await_recv(pool_of_half(0), od_r.at[0])

    def project(half):
        first = (h if half == 0 else 1 - h) * NX
        rows = pl.ds(pl.multiple_of(first * 128, 512), 512)
        lhs = jnp.concatenate(
            [jnp.concatenate([pooled[i, first + s] for s in range(NX)], axis=1) for i in range(2)], axis=0
        )
        return jnp.dot(lhs, proj_perm[rows, :], preferred_element_type=jnp.float32)

    half_sum = project(0)
    for i in range(2):
        by_image[i] = half_sum[144 * i : 144 * (i + 1)]
    @pl.when(c == 1)
    def _():
        pool_to_first(1)

    @pl.when(c == 0)
    def _():
        await_recv(pool_of_half(1), od_r.at[1])

    half_sum = project(1)
    for i in range(2):
        by_image[i] += half_sum[144 * i : 144 * (i + 1)]
    results = []
    for slot in range(2):
        result[slot] = by_image[slot_ref[slot]].astype(jnp.bfloat16)
        results.append(pltpu.make_async_copy(result.at[slot], out_ref.at[slot], loc.at[slot]))
        results[-1].start()

    ce_conv.wait_send()
    ce_img.wait_send()
    await_send(weights.at[pl.ds(0, (NZ - 1 + (NY - 1) * NZ + NY * NZ) * 144)], w_s)
    await_send(grid_img.at[pl.ds(0, (2 * (NX - 1) + 1) * BODY_ROWS)], img_s)
    await_send(rests.at[pl.ds(0, 2 * (NX - 1) + 1)], rest_s)
    await_send(proj_all.at[c, pl.ds(0, 2 * (NX - 1) + 1)], proj_s)
    await_send(proj_all.at[c], proj_cs)
    await_send(proj_cols.at[pl.ds(0, NZ - 1 + (NY - 1) * NZ)], q_s)
    @pl.when(c == 0)
    def _():
        await_send(pooled.at[0, pl.ds(0, NX)], pool_s)
        await_send(own_pool, pool_cs)

    @pl.when(c == 1)
    def _():
        await_send(pooled.at[:, pl.ds(0, (3 * (NX - 1) + 1) // 2)], pool_s)
        await_send(pooled, pool_cs)

    for copy in results:
        copy.wait()


def per_device(patches, image_slot, trainer_blocks, conv_weight, proj_weight):
    dma = pltpu.SemaphoreType.DMA
    anywhere = pl.BlockSpec(memory_space=pl.ANY)
    bf16, f32 = jnp.bfloat16, jnp.float32
    sems = [
        dma((2,)),
        dma,
        dma,
        dma,
        dma,
        dma,
        dma,
        dma,
        dma,
        dma((2,)),
        dma((NZ - 1,)),
        dma((2 * (NY - 1),)),
        dma,
        dma((len(CUTS),)),
        dma((2,)),
        dma,
        dma((2,)),
        dma,
        dma,
        dma,
        dma((NZ - 1,)),
        dma,
        dma((2,)),
        dma((2,)),
        dma,
        dma((2,)),
    ]
    return pl.pallas_call(
        kernel,
        out_shape=jax.ShapeDtypeStruct((2, 144, 512), bf16),
        in_specs=[pl.BlockSpec(memory_space=pltpu.HBM)] * 5,
        out_specs=anywhere,
        scratch_shapes=[
            pltpu.SMEM((16,), jnp.int32),
            pltpu.SMEM((2,), jnp.int32),
            pltpu.VMEM((2, 36, 2, 1024), bf16),
            pltpu.VMEM((2, 64, 288), bf16),
            pltpu.VMEM((288, 128), bf16),
            pltpu.VMEM((SLOTS * SLOT_ROWS, 1024), bf16),
            pltpu.VMEM((SLOTS, 16, 512), bf16),
            pltpu.VMEM((10 * 1024, 128), bf16),
            pltpu.VMEM((10, SLOTS * SLOT_ROWS, 128), f32),
            pltpu.VMEM((288, 128), f32),
            pltpu.VMEM((2, SLOTS, 144, 128), bf16),
            pltpu.VMEM((2, SLOTS, 32, 512), bf16),
            pltpu.VMEM((NY * NZ, 32, 512), bf16),
            pltpu.VMEM((1024, 512), bf16),
            pltpu.VMEM((144, 128), bf16),
            pltpu.VMEM((2, 144, 512), f32),
            pltpu.VMEM((2, 144, 512), bf16),
            pltpu.SemaphoreType.REGULAR,
            pltpu.SemaphoreType.REGULAR,
            dma((5,)),
        ]
        + sems,
        compiler_params=pltpu.CompilerParams(
            collective_id=0, has_side_effects=True, vmem_limit_bytes=40 * 1024 * 1024
        ),
        cost_estimate=pl.CostEstimate(flops=2_000_000_000, bytes_accessed=600_000, transcendentals=73728),
        name="vision",
    )(*(pltpu.with_memory_space_constraint(a, pltpu.HBM) for a in (trainer_blocks, image_slot, jnp.transpose(patches, (1, 0, 2)), conv_weight.T, proj_weight)))


def solution(mesh):
    placed = (P("dp", "tp", None), P("dp"), P(), P("dp", "tp"), P("dp", "tp"))
    return jax.shard_map(
        per_device, mesh=mesh, in_specs=placed, out_specs=P("dp", None, "tp"), check_vma=False
    )
```

```python
import functools

import jax
import jax.numpy as jnp
from jax import lax
from jax.experimental import pallas as pl
from jax.experimental.pallas import tpu as pltpu
from jax.sharding import PartitionSpec as P

MESH = pl.DeviceIdType.MESH

GRID = 24
NX, NY, NZ = 4, 4, 8
SLOTS = 2 * NX
SLOT_ROWS = 80
CHIP_ROWS = 72
BODY_ROWS = 64
CUTS = ((0, 32), (32, 32))


class Place:
    def __init__(self):
        d = lax.axis_index("dp")
        t = lax.axis_index("tp")
        self.y, self.z = d // NZ, lax.rem(d, NZ)
        self.h, self.x, self.c = t // (2 * NX), lax.rem(t // 2, NX), lax.rem(t, 2)
        self.d, self.t = d, t
        self.slot = self.h * NX + self.x

    def at(self, y=None, z=None, h=None, x=None, c=None):
        y = self.y if y is None else y
        z = self.z if z is None else z
        h = self.h if h is None else h
        x = self.x if x is None else x
        c = self.c if c is None else c
        return (y * NZ + z, h * (2 * NX) + x * 2 + c)

    def sibling(self):
        return self.at(c=1 - self.c)

    def flip(self):
        return self.at(h=1 - self.h)


def plus(value, step, size):
    return lax.rem(value + step, size)


def kernel(
    tb_in,
    slot_in,
    patches,
    conv,
    proj,
    out_ref,
    tb_ref,
    slot_ref,
    tokens,
    halves,
    pair_rows,
    grid_img,
    rests,
    weights,
    z_ref,
    fs_ref,
    pooled,
    proj_all,
    proj_cols,
    proj_perm,
    own_pool,
    by_image,
    result,
    half_ok,
    flip_ok,
    loc,
    ce_s,
    w_s,
    img_s,
    rest_s,
    proj_s,
    proj_cs,
    q_s,
    pool_s,
    pool_cs,
    ce_r,
    wz_r,
    wy_r,
    wd_r,
    gz_r,
    gx_r,
    rz_r,
    rx_r,
    pz_r,
    px_r,
    pd_r,
    qz_r,
    qy_r,
    oz_r,
    ox_r,
    oc_r,
    od_r,
):
    me = Place()
    c, h, x, y, z, d = me.c, me.h, me.x, me.y, me.z, me.d
    other = 1 - c
    sibling, flip = me.sibling(), me.flip()
    my_slot = me.slot
    flip_slot = (1 - h) * NX + x

    def remote(src, dst, send, recv, where):
        return pltpu.make_async_remote_copy(
            src_ref=src, dst_ref=dst, send_sem=send, recv_sem=recv, device_id=where, device_id_type=MESH
        )

    def await_recv(dst, recv):
        remote(dst, dst, recv, recv, sibling).wait_recv()

    def await_send(src, send):
        remote(src, src, send, send, sibling).wait_send()

    bits = (lax.rem(z, 2), lax.rem(z // 2, 2), z // 4)

    def across(m):
        return sum((1 - bit if m >> i & 1 else bit) * (1 << i) for i, bit in enumerate(bits))

    barrier = pltpu.get_barrier_semaphore()

    def greet(where):
        pl.semaphore_signal(barrier, inc=1, device_id=where, device_id_type=MESH)

    for k in range(1, NZ):
        greet(me.at(z=plus(z, k, NZ), c=1))
    for k in range(1, NX):
        greet(me.at(x=plus(x, k, NX), c=1))
    for k in range(1, NY):
        greet(me.at(y=plus(y, k, NY), c=1))

    @pl.when(c == 0)
    def _():
        greet(sibling)

    greet(me.at(h=1 - h, c=0))

    local = [
        pltpu.make_async_copy(patches, tokens.at[c], loc.at[0]),
        pltpu.make_async_copy(conv, halves.at[c], loc.at[1]),
        pltpu.make_async_copy(proj, proj_all.at[c, my_slot], loc.at[2]),
        pltpu.make_async_copy(tb_in, tb_ref, loc.at[3]),
        pltpu.make_async_copy(slot_in, slot_ref, loc.at[4]),
    ]
    for copy in local:
        copy.start()

    for copy in local:
        copy.wait()
    @pl.when(c == 1)
    def _():
        pl.semaphore_wait(barrier, 2 * (NZ - 1 + NX - 1 + NY - 1) + 1)
        pl.semaphore_signal(half_ok, inc=1, device_id=sibling, device_id_type=MESH)

    @pl.when(c == 0)
    def _():
        pl.semaphore_wait(half_ok, 1)

    def meet_other_half():
        @pl.when(c == 0)
        def _():
            pl.semaphore_wait(barrier, 2)
            pl.semaphore_signal(flip_ok, inc=1, device_id=sibling, device_id_type=MESH)

        @pl.when(c == 1)
        def _():
            pl.semaphore_wait(flip_ok, 1)


    ce_conv = remote(halves.at[c], halves.at[c], ce_s.at[0], ce_r.at[0], sibling)
    ce_conv.start()
    ce_img = remote(tokens.at[c], tokens.at[c], ce_s.at[1], ce_r.at[1], sibling)
    ce_img.start()
    own_proj = proj_all.at[c, my_slot]
    flip_proj = proj_all.at[c, flip_slot]

    def to_x(piece, send, recv):
        for k in range(1, NX):
            remote(piece, piece, send, recv, me.at(x=plus(x, k, NX))).start()

    def shard(dp, core):
        return weights.at[pl.ds(pl.multiple_of(dp * 288 + core * 144, 16), 144)]

    def w_piece(m, j=0):
        return shard(plus(y, NY - j, NY) * NZ + across(m), c)

    def q_piece(m, j=0):
        return proj_cols.at[plus(y, NY - j, NY) * NZ + across(m)]

    def to_z(piece, m, send, recvs, partners):
        for p in partners:
            remote(piece(m), piece(m), send, recvs.at[(m ^ p) - 1], me.at(z=across(p))).start()

    def w_to_sibling(m, j):
        remote(w_piece(m, j), w_piece(m, j), w_s, wd_r, sibling).start()

    def w_step(m, partners):
        if m:
            await_recv(w_piece(m), wz_r.at[m - 1])
        to_z(w_piece, m, w_s, wz_r, partners)
        for j in range(1, NY):
            remote(w_piece(m), w_piece(m), w_s, wy_r.at[2 * (j - 1) + m % 2], me.at(y=plus(y, j, NY))).start()
        w_to_sibling(m, 0)

    def w_rest(j, odd):
        await_recv(weights.at[pl.ds(0, 4 * 144)], wy_r.at[2 * (j - 1) + odd])
        for m in range(odd, NZ, 2):
            w_to_sibling(m, j)

    def q_step(m, partners):
        if m:
            await_recv(q_piece(m), qz_r.at[m - 1])
        to_z(q_piece, m, q_s, qz_r, partners)
        for j in range(1, NY):
            remote(q_piece(m), q_piece(m), q_s, qy_r, me.at(y=plus(y, j, NY))).start()

    def proj_along_x():
        await_recv(flip_proj, pz_r)
        to_x(flip_proj, proj_s, px_r)

    def proj_to_sibling():
        await_recv(proj_all.at[c, pl.ds(0, 2 * (NX - 1))], px_r)
        remote(proj_all.at[c], proj_all.at[c], proj_cs, pd_r, sibling).start()

    def proj_select():
        await_recv(proj_all.at[other], pd_r)
        holder = jnp.int32(0)
        for t in range(4 * NX):
            holder = jnp.where(tb_ref[t] == me.t, t, holder)
        q_piece(0)[...] = proj_all[lax.rem(holder, 2), holder // 2]

    await_recv(halves.at[other], ce_r.at[0])
    own_shard = w_piece(0)
    both = jnp.concatenate([halves[0], halves[1]], axis=0).astype(jnp.float32)
    both = jnp.concatenate([both, jnp.zeros((128, 96), jnp.float32)], axis=1)
    pair_rows[...] = both.T[:288].astype(jnp.bfloat16)
    own_shard[...] = pair_rows[pl.ds(pl.multiple_of(c * 144, 16), 144), :]
    w_step(0, (4, 2, 1))
    to_x(own_proj, proj_s, px_r)

    @pl.when(h == 1)
    def _():
        meet_other_half()
        remote(own_proj, own_proj, proj_s, pz_r, flip).start()


    await_recv(tokens.at[other], ce_r.at[1])
    mine = [
        jnp.where(c == 0, both[:, 0, :], both[:, 1, :]) for both in (tokens[i].astype(jnp.float32) for i in range(2))
    ]
    chip_tokens = jnp.concatenate(mine + [jnp.zeros((SLOT_ROWS - CHIP_ROWS, 1024), jnp.float32)], axis=0)

    def image(slot, first=0, count=SLOT_ROWS):
        return grid_img.at[pl.ds(pl.multiple_of(slot * SLOT_ROWS + first, 16), count)]

    image(my_slot, 0, BODY_ROWS)[...] = chip_tokens[:BODY_ROWS].astype(jnp.bfloat16)
    own_rest = chip_tokens[BODY_ROWS:CHIP_ROWS]
    rests[my_slot] = jnp.concatenate([own_rest[:, :512], own_rest[:, 512:]], axis=0).astype(jnp.bfloat16)
    to_x(image(my_slot, 0, BODY_ROWS), img_s, gx_r.at[0])
    to_x(rests.at[my_slot], rest_s, rx_r.at[0])

    def flip_cut(i):
        piece = image(my_slot, *CUTS[i])
        remote(piece, piece, img_s, gz_r.at[i], flip).start()

    def flip_rest():
        remote(rests.at[my_slot], rests.at[my_slot], rest_s, rz_r, flip).start()

    def image_step(i):
        piece = image(flip_slot, *CUTS[i])
        await_recv(piece, gz_r.at[i])
        to_x(piece, img_s, gx_r.at[1])

    def rest_step():
        await_recv(rests.at[flip_slot], rz_r)
        to_x(rests.at[flip_slot], rest_s, rx_r.at[1])

    def image_wait(which):
        await_recv(grid_img.at[pl.ds(0, (NX - 1) * BODY_ROWS)], gx_r.at[which])
        await_recv(rests.at[pl.ds(0, NX - 1)], rx_r.at[which])

    def put_rests(half):
        for i in range(NX):
            rest = rests[half * NX + i].astype(jnp.float32)
            rest = jnp.concatenate([rest[:8], rest[8:]], axis=1)
            rest = jnp.concatenate([rest, jnp.zeros((8, 1024), jnp.float32)], axis=0)
            image(half * NX + i, BODY_ROWS, 16)[...] = rest.astype(jnp.bfloat16)

    def multiply(half):
        put_rests(half)
        rows = pl.ds(pl.multiple_of(half * (NX * SLOT_ROWS), 64), NX * SLOT_ROWS)

        @pl.loop(0, 5)
        def _(n):
            rhs = jnp.concatenate(
                [
                    weights[pl.ds(pl.multiple_of(n * 2048, 1024), 1024), :],
                    weights[pl.ds(pl.multiple_of(n * 2048 + 1024, 1024), 1024), :],
                ],
                axis=1,
            )
            prod = jnp.dot(grid_img[rows, :], rhs, preferred_element_type=jnp.float32)
            z_ref[2 * n, rows, :] = prod[:, :128]
            z_ref[2 * n + 1, rows, :] = prod[:, 128:]

    @pl.when(h == 0)
    def _():
        meet_other_half()
        remote(own_proj, own_proj, proj_s, pz_r, flip).start()

    row = lax.broadcasted_iota(jnp.int32, (1024, 128), 0)
    lane = lax.broadcasted_iota(jnp.int32, (1024, 128), 1)
    first = tb_ref[2 * my_slot] * 64
    second = tb_ref[2 * my_slot + 1] * 64 - 64
    wanted = lane + jnp.where(lane < 64, first, second)
    weights[pl.ds(9 * 1024, 1024), :] = jnp.where(row == wanted, 1.0, 0.0).astype(jnp.bfloat16)
    w_step(4, (2, 1))
    @pl.when(h == 1)
    def _():
        flip_cut(0)

    @pl.when(h == 0)
    def _():
        flip_cut(0)
        flip_cut(1)
        flip_rest()

    w_step(2, (1,))
    w_step(6, (1,))
    @pl.when(h == 1)
    def _():
        flip_cut(1)
        flip_rest()

    proj_along_x()
    w_step(1, ())
    w_step(5, ())
    proj_to_sibling()
    @pl.when(h == 0)
    def _():
        proj_select()
        q_step(0, (4, 1, 2, 3))

    @pl.when(h == 1)
    def _():
        image_step(0)

    w_step(3, ())
    w_step(7, ())
    @pl.when(h == 1)
    def _():
        proj_select()
        q_step(0, (4, 2, 1))


    @pl.when(h == 0)
    def _():
        image_step(0)

    for j in range(1, NY):
        w_rest(j, 0)
    image_step(1)
    rest_step()
    @pl.when(h == 0)
    def _():
        q_step(4, (1, 2, 3))

    @pl.when(h == 0)
    def _():
        for m in (1, 2, 3):
            q_step(m, ())

    for j in range(1, NY):
        w_rest(j, 1)
    await_recv(weights.at[pl.ds(0, NY * NZ * 144)], wd_r)
    image_wait(0)
    multiply(h)
    image_wait(1)
    @pl.when(h == 0)
    def _():
        for m in (5, 6, 7):
            q_step(m, ())

    multiply(1 - h)

    column = lax.broadcasted_iota(jnp.int32, (GRID, 128), 0)

    def product(tap, gy):
        return z_ref[tap, pl.ds((gy // 3) * SLOT_ROWS + (gy % 3) * GRID, GRID), :]

    for gy in range(0, GRID, 2):
        total = jnp.zeros((GRID, 128), jnp.float32)
        for row_y in (gy, gy + 1):
            parts = []
            for kx in range(3):
                part = None
                for ky in range(3):
                    if 0 <= row_y + ky - 1 < GRID:
                        value = product(3 * ky + kx, row_y + ky - 1)
                        part = value if part is None else part + value
                parts.append(part)
            left = jnp.where(column == 0, 0.0, pltpu.roll(parts[0], 1, 0))
            right = jnp.where(column == GRID - 1, 0.0, pltpu.roll(parts[2], GRID - 1, 0))
            value = parts[1] + left + right
            total = total + product(9, row_y) + value / (1.0 + jnp.exp(-value))
        fs_ref[pl.ds((gy // 2) * GRID, GRID), :] = total
    mean = (fs_ref[pl.ds(0, 144, stride=2), :] + fs_ref[pl.ds(1, 144, stride=2), :]) * 0.25
    own_pool[...] = mean.astype(jnp.bfloat16)

    def pool_to_x(piece, dst, half):
        for k in range(1, NX):
            remote(piece, dst, pool_s, ox_r.at[half], me.at(x=plus(x, k, NX), c=1)).start()

    remote(own_pool, pooled.at[c, my_slot], pool_s, oz_r.at[c], me.at(h=1 - h, c=1)).start()
    pool_to_x(own_pool, pooled.at[c, my_slot], 0)

    @pl.when(c == 0)
    def _():
        remote(own_pool, pooled.at[0, my_slot], pool_cs, oc_r, sibling).start()

    @pl.when(c == 1)
    def _():
        pooled[1, my_slot] = own_pool[...]

    @pl.when(h == 1)
    def _():
        q_step(4, (2, 1))

    @pl.when(h == 1)
    def _():
        q_step(2, (1,))
        q_step(6, (1,))

    @pl.when(h == 1)
    def _():
        for m in (1, 5, 3, 7):
            q_step(m, ())

    @pl.when(c == 1)
    def _():
        for i in (1, 0):
            flip_pool = pooled.at[i, flip_slot]
            await_recv(flip_pool, oz_r.at[i])
            pool_to_x(flip_pool, flip_pool, 1)

    def pool_of_half(half):
        return pooled.at[:, pl.ds((h if half == 0 else 1 - h) * NX, NX)]

    def pool_to_first(half):
        await_recv(pooled.at[:, pl.ds(0, NX - 1)], ox_r.at[half])
        remote(pool_of_half(half), pool_of_half(half), pool_cs, od_r.at[half], sibling).start()

    @pl.when(c == 1)
    def _():
        await_recv(pooled.at[0, my_slot], oc_r)
        pool_to_first(0)

    await_recv(proj_cols.at[pl.ds(0, (NY - 1) * NZ)], qy_r)

    for t in range(4 * NX):
        block = tb_ref[t]
        proj_perm[pl.ds(t * 64, 32), :] = proj_cols[2 * block]
        proj_perm[pl.ds(t * 64 + 32, 32), :] = proj_cols[2 * block + 1]

    @pl.when(c == 0)
    def _():
        await_recv(pool_of_half(0), od_r.at[0])

    def project(half):
        first = (h if half == 0 else 1 - h) * NX
        rows = pl.ds(pl.multiple_of(first * 128, 512), 512)
        lhs = jnp.concatenate(
            [jnp.concatenate([pooled[i, first + s] for s in range(NX)], axis=1) for i in range(2)], axis=0
        )
        return jnp.dot(lhs, proj_perm[rows, :], preferred_element_type=jnp.float32)

    half_sum = project(0)
    for i in range(2):
        by_image[i] = half_sum[144 * i : 144 * (i + 1)]
    @pl.when(c == 1)
    def _():
        pool_to_first(1)

    @pl.when(c == 0)
    def _():
        await_recv(pool_of_half(1), od_r.at[1])

    half_sum = project(1)
    for i in range(2):
        by_image[i] += half_sum[144 * i : 144 * (i + 1)]
    results = []
    for slot in range(2):
        result[slot] = by_image[slot_ref[slot]].astype(jnp.bfloat16)
        results.append(pltpu.make_async_copy(result.at[slot], out_ref.at[slot], loc.at[slot]))
        results[-1].start()

    ce_conv.wait_send()
    ce_img.wait_send()
    await_send(weights.at[pl.ds(0, (NZ - 1 + (NY - 1) * NZ + NY * NZ) * 144)], w_s)
    await_send(grid_img.at[pl.ds(0, (2 * (NX - 1) + 1) * BODY_ROWS)], img_s)
    await_send(rests.at[pl.ds(0, 2 * (NX - 1) + 1)], rest_s)
    await_send(proj_all.at[c, pl.ds(0, 2 * (NX - 1) + 1)], proj_s)
    await_send(proj_all.at[c], proj_cs)
    await_send(proj_cols.at[pl.ds(0, NZ - 1 + (NY - 1) * NZ)], q_s)
    @pl.when(c == 0)
    def _():
        await_send(pooled.at[0, pl.ds(0, NX)], pool_s)
        await_send(own_pool, pool_cs)

    @pl.when(c == 1)
    def _():
        await_send(pooled.at[:, pl.ds(0, (3 * (NX - 1) + 1) // 2)], pool_s)
        await_send(pooled, pool_cs)

    for copy in results:
        copy.wait()


def per_device(patches, image_slot, trainer_blocks, conv_weight, proj_weight):
    dma = pltpu.SemaphoreType.DMA
    anywhere = pl.BlockSpec(memory_space=pl.ANY)
    bf16, f32 = jnp.bfloat16, jnp.float32
    sems = [
        dma((2,)),
        dma,
        dma,
        dma,
        dma,
        dma,
        dma,
        dma,
        dma,
        dma((2,)),
        dma((NZ - 1,)),
        dma((2 * (NY - 1),)),
        dma,
        dma((len(CUTS),)),
        dma((2,)),
        dma,
        dma((2,)),
        dma,
        dma,
        dma,
        dma((NZ - 1,)),
        dma,
        dma((2,)),
        dma((2,)),
        dma,
        dma((2,)),
    ]
    return pl.pallas_call(
        kernel,
        out_shape=jax.ShapeDtypeStruct((2, 144, 512), bf16),
        in_specs=[pl.BlockSpec(memory_space=pltpu.HBM)] * 5,
        out_specs=anywhere,
        scratch_shapes=[
            pltpu.SMEM((16,), jnp.int32),
            pltpu.SMEM((2,), jnp.int32),
            pltpu.VMEM((2, 36, 2, 1024), bf16),
            pltpu.VMEM((2, 64, 288), bf16),
            pltpu.VMEM((288, 128), bf16),
            pltpu.VMEM((SLOTS * SLOT_ROWS, 1024), bf16),
            pltpu.VMEM((SLOTS, 16, 512), bf16),
            pltpu.VMEM((10 * 1024, 128), bf16),
            pltpu.VMEM((10, SLOTS * SLOT_ROWS, 128), f32),
            pltpu.VMEM((288, 128), f32),
            pltpu.VMEM((2, SLOTS, 144, 128), bf16),
            pltpu.VMEM((2, SLOTS, 32, 512), bf16),
            pltpu.VMEM((NY * NZ, 32, 512), bf16),
            pltpu.VMEM((1024, 512), bf16),
            pltpu.VMEM((144, 128), bf16),
            pltpu.VMEM((2, 144, 512), f32),
            pltpu.VMEM((2, 144, 512), bf16),
            pltpu.SemaphoreType.REGULAR,
            pltpu.SemaphoreType.REGULAR,
            dma((5,)),
        ]
        + sems,
        compiler_params=pltpu.CompilerParams(
            collective_id=0, has_side_effects=True, vmem_limit_bytes=40 * 1024 * 1024
        ),
        cost_estimate=pl.CostEstimate(flops=2_000_000_000, bytes_accessed=600_000, transcendentals=73728),
        name="vision",
    )(*(pltpu.with_memory_space_constraint(a, pltpu.HBM) for a in (trainer_blocks, image_slot, jnp.transpose(patches, (1, 0, 2)), conv_weight.T, proj_weight)))


def solution(mesh):
    placed = (P("dp", "tp", None), P("dp"), P(), P("dp", "tp"), P("dp", "tp"))
    return jax.shard_map(
        per_device, mesh=mesh, in_specs=placed, out_specs=P("dp", None, "tp"), check_vma=False
    )
```

```python
import functools

import jax
import jax.numpy as jnp
from jax import lax
from jax.experimental import pallas as pl
from jax.experimental.pallas import tpu as pltpu
from jax.sharding import PartitionSpec as P

MESH = pl.DeviceIdType.MESH

GRID = 24
NX, NY, NZ = 4, 4, 8
SLOTS = 2 * NX
SLOT_ROWS = 80
CHIP_ROWS = 72
BODY_ROWS = 64
CUTS = ((0, 32), (32, 32))


class Place:
    def __init__(self):
        d = lax.axis_index("dp")
        t = lax.axis_index("tp")
        self.y, self.z = d // NZ, lax.rem(d, NZ)
        self.h, self.x, self.c = t // (2 * NX), lax.rem(t // 2, NX), lax.rem(t, 2)
        self.d, self.t = d, t
        self.slot = self.h * NX + self.x

    def at(self, y=None, z=None, h=None, x=None, c=None):
        y = self.y if y is None else y
        z = self.z if z is None else z
        h = self.h if h is None else h
        x = self.x if x is None else x
        c = self.c if c is None else c
        return (y * NZ + z, h * (2 * NX) + x * 2 + c)

    def sibling(self):
        return self.at(c=1 - self.c)

    def flip(self):
        return self.at(h=1 - self.h)


def plus(value, step, size):
    return lax.rem(value + step, size)


def kernel(
    tb_in,
    slot_in,
    patches,
    conv,
    proj,
    out_ref,
    tb_ref,
    slot_ref,
    tokens,
    halves,
    pair_rows,
    grid_img,
    rests,
    weights,
    z_ref,
    fs_ref,
    pooled,
    proj_all,
    proj_cols,
    proj_perm,
    own_pool,
    by_image,
    result,
    half_ok,
    flip_ok,
    loc,
    ce_s,
    w_s,
    img_s,
    rest_s,
    proj_s,
    proj_cs,
    q_s,
    pool_s,
    pool_cs,
    ce_r,
    wz_r,
    wy_r,
    wd_r,
    gz_r,
    gx_r,
    rz_r,
    rx_r,
    pz_r,
    px_r,
    pd_r,
    qz_r,
    qy_r,
    oz_r,
    ox_r,
    oc_r,
    od_r,
):
    me = Place()
    c, h, x, y, z, d = me.c, me.h, me.x, me.y, me.z, me.d
    other = 1 - c
    sibling, flip = me.sibling(), me.flip()
    my_slot = me.slot
    flip_slot = (1 - h) * NX + x

    def remote(src, dst, send, recv, where):
        return pltpu.make_async_remote_copy(
            src_ref=src, dst_ref=dst, send_sem=send, recv_sem=recv, device_id=where, device_id_type=MESH
        )

    def await_recv(dst, recv):
        remote(dst, dst, recv, recv, sibling).wait_recv()

    def await_send(src, send):
        remote(src, src, send, send, sibling).wait_send()

    bits = (lax.rem(z, 2), lax.rem(z // 2, 2), z // 4)

    def across(m):
        return sum((1 - bit if m >> i & 1 else bit) * (1 << i) for i, bit in enumerate(bits))

    barrier = pltpu.get_barrier_semaphore()

    def greet(where):
        pl.semaphore_signal(barrier, inc=1, device_id=where, device_id_type=MESH)

    for k in range(1, NZ):
        greet(me.at(z=plus(z, k, NZ), c=1))
    for k in range(1, NX):
        greet(me.at(x=plus(x, k, NX), c=1))
    for k in range(1, NY):
        greet(me.at(y=plus(y, k, NY), c=1))

    @pl.when(c == 0)
    def _():
        greet(sibling)

    greet(me.at(h=1 - h, c=0))

    local = [
        pltpu.make_async_copy(patches, tokens.at[c], loc.at[0]),
        pltpu.make_async_copy(conv, halves.at[c], loc.at[1]),
        pltpu.make_async_copy(proj, proj_all.at[c, my_slot], loc.at[2]),
        pltpu.make_async_copy(tb_in, tb_ref, loc.at[3]),
        pltpu.make_async_copy(slot_in, slot_ref, loc.at[4]),
    ]
    for copy in local:
        copy.start()

    for copy in local:
        copy.wait()
    @pl.when(c == 1)
    def _():
        pl.semaphore_wait(barrier, 2 * (NZ - 1 + NX - 1 + NY - 1) + 1)
        pl.semaphore_signal(half_ok, inc=1, device_id=sibling, device_id_type=MESH)

    @pl.when(c == 0)
    def _():
        pl.semaphore_wait(half_ok, 1)

    def meet_other_half():
        @pl.when(c == 0)
        def _():
            pl.semaphore_wait(barrier, 2)
            pl.semaphore_signal(flip_ok, inc=1, device_id=sibling, device_id_type=MESH)

        @pl.when(c == 1)
        def _():
            pl.semaphore_wait(flip_ok, 1)


    ce_conv = remote(halves.at[c], halves.at[c], ce_s.at[0], ce_r.at[0], sibling)
    ce_conv.start()
    ce_img = remote(tokens.at[c], tokens.at[c], ce_s.at[1], ce_r.at[1], sibling)
    ce_img.start()
    own_proj = proj_all.at[c, my_slot]
    flip_proj = proj_all.at[c, flip_slot]

    def to_x(piece, send, recv):
        for k in range(1, NX):
            remote(piece, piece, send, recv, me.at(x=plus(x, k, NX))).start()

    def shard(dp, core):
        return weights.at[pl.ds(pl.multiple_of(dp * 288 + core * 144, 16), 144)]

    def w_piece(m, j=0):
        return shard(plus(y, NY - j, NY) * NZ + across(m), c)

    def q_piece(m, j=0):
        return proj_cols.at[plus(y, NY - j, NY) * NZ + across(m)]

    def to_z(piece, m, send, recvs, partners):
        for p in partners:
            remote(piece(m), piece(m), send, recvs.at[(m ^ p) - 1], me.at(z=across(p))).start()

    def w_to_sibling(m, j):
        remote(w_piece(m, j), w_piece(m, j), w_s, wd_r, sibling).start()

    def w_step(m, partners):
        if m:
            await_recv(w_piece(m), wz_r.at[m - 1])
        to_z(w_piece, m, w_s, wz_r, partners)
        for j in range(1, NY):
            remote(w_piece(m), w_piece(m), w_s, wy_r.at[2 * (j - 1) + m % 2], me.at(y=plus(y, j, NY))).start()
        w_to_sibling(m, 0)

    def w_rest(j, odd):
        await_recv(weights.at[pl.ds(0, 4 * 144)], wy_r.at[2 * (j - 1) + odd])
        for m in range(odd, NZ, 2):
            w_to_sibling(m, j)

    def q_step(m, partners):
        if m:
            await_recv(q_piece(m), qz_r.at[m - 1])
        to_z(q_piece, m, q_s, qz_r, partners)
        for j in range(1, NY):
            remote(q_piece(m), q_piece(m), q_s, qy_r, me.at(y=plus(y, j, NY))).start()

    def proj_along_x():
        await_recv(flip_proj, pz_r)
        to_x(flip_proj, proj_s, px_r)

    def proj_to_sibling():
        await_recv(proj_all.at[c, pl.ds(0, 2 * (NX - 1))], px_r)
        remote(proj_all.at[c], proj_all.at[c], proj_cs, pd_r, sibling).start()

    def proj_select():
        await_recv(proj_all.at[other], pd_r)
        holder = jnp.int32(0)
        for t in range(4 * NX):
            holder = jnp.where(tb_ref[t] == me.t, t, holder)
        q_piece(0)[...] = proj_all[lax.rem(holder, 2), holder // 2]

    await_recv(halves.at[other], ce_r.at[0])
    own_shard = w_piece(0)
    both = jnp.concatenate([halves[0], halves[1]], axis=0).astype(jnp.float32)
    both = jnp.concatenate([both, jnp.zeros((128, 96), jnp.float32)], axis=1)
    pair_rows[...] = both.T[:288].astype(jnp.bfloat16)
    own_shard[...] = pair_rows[pl.ds(pl.multiple_of(c * 144, 16), 144), :]
    w_step(0, (4, 2, 1))
    to_x(own_proj, proj_s, px_r)

    @pl.when(h == 1)
    def _():
        meet_other_half()
        remote(own_proj, own_proj, proj_s, pz_r, flip).start()


    await_recv(tokens.at[other], ce_r.at[1])
    mine = [
        jnp.where(c == 0, both[:, 0, :], both[:, 1, :]) for both in (tokens[i].astype(jnp.float32) for i in range(2))
    ]
    chip_tokens = jnp.concatenate(mine + [jnp.zeros((SLOT_ROWS - CHIP_ROWS, 1024), jnp.float32)], axis=0)

    def image(slot, first=0, count=SLOT_ROWS):
        return grid_img.at[pl.ds(pl.multiple_of(slot * SLOT_ROWS + first, 16), count)]

    image(my_slot, 0, BODY_ROWS)[...] = chip_tokens[:BODY_ROWS].astype(jnp.bfloat16)
    own_rest = chip_tokens[BODY_ROWS:CHIP_ROWS]
    rests[my_slot] = jnp.concatenate([own_rest[:, :512], own_rest[:, 512:]], axis=0).astype(jnp.bfloat16)
    to_x(image(my_slot, 0, BODY_ROWS), img_s, gx_r.at[0])
    to_x(rests.at[my_slot], rest_s, rx_r.at[0])

    def flip_cut(i):
        piece = image(my_slot, *CUTS[i])
        remote(piece, piece, img_s, gz_r.at[i], flip).start()

    def flip_rest():
        remote(rests.at[my_slot], rests.at[my_slot], rest_s, rz_r, flip).start()

    def image_step(i):
        piece = image(flip_slot, *CUTS[i])
        await_recv(piece, gz_r.at[i])
        to_x(piece, img_s, gx_r.at[1])

    def rest_step():
        await_recv(rests.at[flip_slot], rz_r)
        to_x(rests.at[flip_slot], rest_s, rx_r.at[1])

    def image_wait(which):
        await_recv(grid_img.at[pl.ds(0, (NX - 1) * BODY_ROWS)], gx_r.at[which])
        await_recv(rests.at[pl.ds(0, NX - 1)], rx_r.at[which])

    def put_rests(half):
        for i in range(NX):
            rest = rests[half * NX + i].astype(jnp.float32)
            rest = jnp.concatenate([rest[:8], rest[8:]], axis=1)
            rest = jnp.concatenate([rest, jnp.zeros((8, 1024), jnp.float32)], axis=0)
            image(half * NX + i, BODY_ROWS, 16)[...] = rest.astype(jnp.bfloat16)

    def multiply(half):
        put_rests(half)
        rows = pl.ds(pl.multiple_of(half * (NX * SLOT_ROWS), 64), NX * SLOT_ROWS)

        @pl.loop(0, 5)
        def _(n):
            rhs = jnp.concatenate(
                [
                    weights[pl.ds(pl.multiple_of(n * 2048, 1024), 1024), :],
                    weights[pl.ds(pl.multiple_of(n * 2048 + 1024, 1024), 1024), :],
                ],
                axis=1,
            )
            prod = jnp.dot(grid_img[rows, :], rhs, preferred_element_type=jnp.float32)
            z_ref[2 * n, rows, :] = prod[:, :128]
            z_ref[2 * n + 1, rows, :] = prod[:, 128:]

    @pl.when(h == 0)
    def _():
        meet_other_half()
        remote(own_proj, own_proj, proj_s, pz_r, flip).start()

    row = lax.broadcasted_iota(jnp.int32, (1024, 128), 0)
    lane = lax.broadcasted_iota(jnp.int32, (1024, 128), 1)
    first = tb_ref[2 * my_slot] * 64
    second = tb_ref[2 * my_slot + 1] * 64 - 64
    wanted = lane + jnp.where(lane < 64, first, second)
    weights[pl.ds(9 * 1024, 1024), :] = jnp.where(row == wanted, 1.0, 0.0).astype(jnp.bfloat16)
    w_step(4, (2, 1))
    @pl.when(h == 1)
    def _():
        flip_cut(0)

    @pl.when(h == 0)
    def _():
        flip_cut(0)
        flip_cut(1)
        flip_rest()

    w_step(2, (1,))
    w_step(6, (1,))
    @pl.when(h == 1)
    def _():
        flip_cut(1)
        flip_rest()

    proj_along_x()
    w_step(1, ())
    w_step(5, ())
    proj_to_sibling()
    @pl.when(h == 0)
    def _():
        proj_select()
        q_step(0, (4, 1, 2, 3))

    @pl.when(h == 1)
    def _():
        image_step(0)

    w_step(3, ())
    w_step(7, ())
    @pl.when(h == 1)
    def _():
        proj_select()
        q_step(0, (4, 2, 1))


    @pl.when(h == 0)
    def _():
        image_step(0)

    for j in range(1, NY):
        w_rest(j, 0)
    image_step(1)
    rest_step()
    @pl.when(h == 0)
    def _():
        q_step(4, (1, 2, 3))

    @pl.when(h == 0)
    def _():
        for m in (1, 2, 3):
            q_step(m, ())

    for j in range(1, NY):
        w_rest(j, 1)
    await_recv(weights.at[pl.ds(0, NY * NZ * 144)], wd_r)
    image_wait(0)
    multiply(h)
    image_wait(1)
    @pl.when(h == 0)
    def _():
        for m in (5, 6, 7):
            q_step(m, ())

    multiply(1 - h)

    column = lax.broadcasted_iota(jnp.int32, (GRID, 128), 0)

    def product(tap, gy):
        return z_ref[tap, pl.ds((gy // 3) * SLOT_ROWS + (gy % 3) * GRID, GRID), :]

    for gy in range(0, GRID, 2):
        total = jnp.zeros((GRID, 128), jnp.float32)
        for row_y in (gy, gy + 1):
            parts = []
            for kx in range(3):
                part = None
                for ky in range(3):
                    if 0 <= row_y + ky - 1 < GRID:
                        value = product(3 * ky + kx, row_y + ky - 1)
                        part = value if part is None else part + value
                parts.append(part)
            left = jnp.where(column == 0, 0.0, pltpu.roll(parts[0], 1, 0))
            right = jnp.where(column == GRID - 1, 0.0, pltpu.roll(parts[2], GRID - 1, 0))
            value = parts[1] + left + right
            total = total + product(9, row_y) + value / (1.0 + jnp.exp(-value))
        fs_ref[pl.ds((gy // 2) * GRID, GRID), :] = total
    mean = (fs_ref[pl.ds(0, 144, stride=2), :] + fs_ref[pl.ds(1, 144, stride=2), :]) * 0.25
    own_pool[...] = mean.astype(jnp.bfloat16)

    def pool_to_x(piece, dst, half):
        for k in range(1, NX):
            remote(piece, dst, pool_s, ox_r.at[half], me.at(x=plus(x, k, NX), c=1)).start()

    remote(own_pool, pooled.at[c, my_slot], pool_s, oz_r.at[c], me.at(h=1 - h, c=1)).start()
    pool_to_x(own_pool, pooled.at[c, my_slot], 0)

    @pl.when(c == 0)
    def _():
        remote(own_pool, pooled.at[0, my_slot], pool_cs, oc_r, sibling).start()

    @pl.when(c == 1)
    def _():
        pooled[1, my_slot] = own_pool[...]

    @pl.when(h == 1)
    def _():
        q_step(4, (2, 1))

    @pl.when(h == 1)
    def _():
        q_step(2, (1,))
        q_step(6, (1,))

    @pl.when(h == 1)
    def _():
        for m in (1, 5, 3, 7):
            q_step(m, ())

    @pl.when(c == 1)
    def _():
        for i in (1, 0):
            flip_pool = pooled.at[i, flip_slot]
            await_recv(flip_pool, oz_r.at[i])
            pool_to_x(flip_pool, flip_pool, 1)

    def pool_of_half(half):
        return pooled.at[:, pl.ds((h if half == 0 else 1 - h) * NX, NX)]

    def pool_to_first(half):
        await_recv(pooled.at[:, pl.ds(0, NX - 1)], ox_r.at[half])
        remote(pool_of_half(half), pool_of_half(half), pool_cs, od_r.at[half], sibling).start()

    @pl.when(c == 1)
    def _():
        await_recv(pooled.at[0, my_slot], oc_r)
        pool_to_first(0)

    await_recv(proj_cols.at[pl.ds(0, (NY - 1) * NZ)], qy_r)

    for t in range(4 * NX):
        block = tb_ref[t]
        proj_perm[pl.ds(t * 64, 32), :] = proj_cols[2 * block]
        proj_perm[pl.ds(t * 64 + 32, 32), :] = proj_cols[2 * block + 1]

    @pl.when(c == 0)
    def _():
        await_recv(pool_of_half(0), od_r.at[0])

    def project(half):
        first = (h if half == 0 else 1 - h) * NX
        rows = pl.ds(pl.multiple_of(first * 128, 512), 512)
        lhs = jnp.concatenate(
            [jnp.concatenate([pooled[i, first + s] for s in range(NX)], axis=1) for i in range(2)], axis=0
        )
        return jnp.dot(lhs, proj_perm[rows, :], preferred_element_type=jnp.float32)

    half_sum = project(0)
    for i in range(2):
        by_image[i] = half_sum[144 * i : 144 * (i + 1)]
    @pl.when(c == 1)
    def _():
        pool_to_first(1)

    @pl.when(c == 0)
    def _():
        await_recv(pool_of_half(1), od_r.at[1])

    half_sum = project(1)
    for i in range(2):
        by_image[i] += half_sum[144 * i : 144 * (i + 1)]
    results = []
    for slot in range(2):
        result[slot] = by_image[slot_ref[slot]].astype(jnp.bfloat16)
        results.append(pltpu.make_async_copy(result.at[slot], out_ref.at[slot], loc.at[slot]))
        results[-1].start()

    ce_conv.wait_send()
    ce_img.wait_send()
    await_send(weights.at[pl.ds(0, (NZ - 1 + (NY - 1) * NZ + NY * NZ) * 144)], w_s)
    await_send(grid_img.at[pl.ds(0, (2 * (NX - 1) + 1) * BODY_ROWS)], img_s)
    await_send(rests.at[pl.ds(0, 2 * (NX - 1) + 1)], rest_s)
    await_send(proj_all.at[c, pl.ds(0, 2 * (NX - 1) + 1)], proj_s)
    await_send(proj_all.at[c], proj_cs)
    await_send(proj_cols.at[pl.ds(0, NZ - 1 + (NY - 1) * NZ)], q_s)
    @pl.when(c == 0)
    def _():
        await_send(pooled.at[0, pl.ds(0, NX)], pool_s)
        await_send(own_pool, pool_cs)

    @pl.when(c == 1)
    def _():
        await_send(pooled.at[:, pl.ds(0, (3 * (NX - 1) + 1) // 2)], pool_s)
        await_send(pooled, pool_cs)

    for copy in results:
        copy.wait()


def per_device(patches, image_slot, trainer_blocks, conv_weight, proj_weight):
    dma = pltpu.SemaphoreType.DMA
    anywhere = pl.BlockSpec(memory_space=pl.ANY)
    bf16, f32 = jnp.bfloat16, jnp.float32
    sems = [
        dma((2,)),
        dma,
        dma,
        dma,
        dma,
        dma,
        dma,
        dma,
        dma,
        dma((2,)),
        dma((NZ - 1,)),
        dma((2 * (NY - 1),)),
        dma,
        dma((len(CUTS),)),
        dma((2,)),
        dma,
        dma((2,)),
        dma,
        dma,
        dma,
        dma((NZ - 1,)),
        dma,
        dma((2,)),
        dma((2,)),
        dma,
        dma((2,)),
    ]
    return pl.pallas_call(
        kernel,
        out_shape=jax.ShapeDtypeStruct((2, 144, 512), bf16),
        in_specs=[pl.BlockSpec(memory_space=pltpu.HBM)] * 5,
        out_specs=anywhere,
        scratch_shapes=[
            pltpu.SMEM((16,), jnp.int32),
            pltpu.SMEM((2,), jnp.int32),
            pltpu.VMEM((2, 36, 2, 1024), bf16),
            pltpu.VMEM((2, 64, 288), bf16),
            pltpu.VMEM((288, 128), bf16),
            pltpu.VMEM((SLOTS * SLOT_ROWS, 1024), bf16),
            pltpu.VMEM((SLOTS, 16, 512), bf16),
            pltpu.VMEM((10 * 1024, 128), bf16),
            pltpu.VMEM((10, SLOTS * SLOT_ROWS, 128), f32),
            pltpu.VMEM((296, 128), f32),
            pltpu.VMEM((2, SLOTS, 144, 128), bf16),
            pltpu.VMEM((2, SLOTS, 32, 512), bf16),
            pltpu.VMEM((NY * NZ, 32, 512), bf16),
            pltpu.VMEM((1024, 512), bf16),
            pltpu.VMEM((144, 128), bf16),
            pltpu.VMEM((2, 144, 512), f32),
            pltpu.VMEM((2, 144, 512), bf16),
            pltpu.SemaphoreType.REGULAR,
            pltpu.SemaphoreType.REGULAR,
            dma((5,)),
        ]
        + sems,
        compiler_params=pltpu.CompilerParams(
            collective_id=0, has_side_effects=True, vmem_limit_bytes=40 * 1024 * 1024
        ),
        cost_estimate=pl.CostEstimate(flops=2_000_000_000, bytes_accessed=600_000, transcendentals=73728),
        name="vision",
    )(*(pltpu.with_memory_space_constraint(a, pltpu.HBM) for a in (trainer_blocks, image_slot, jnp.transpose(patches, (1, 0, 2)), conv_weight.T, proj_weight)))


def solution(mesh):
    placed = (P("dp", "tp", None), P("dp"), P(), P("dp", "tp"), P("dp", "tp"))
    return jax.shard_map(
        per_device, mesh=mesh, in_specs=placed, out_specs=P("dp", None, "tp"), check_vma=False
    )
```

```python
import functools

import jax
import jax.numpy as jnp
from jax import lax
from jax.experimental import pallas as pl
from jax.experimental.pallas import tpu as pltpu
from jax.sharding import PartitionSpec as P

MESH = pl.DeviceIdType.MESH

GRID = 24
NX, NY, NZ = 4, 4, 8
SLOTS = 2 * NX
SLOT_ROWS = 80
CHIP_ROWS = 72
BODY_ROWS = 64
CUTS = ((0, 32), (32, 32))


class Place:
    def __init__(self):
        d = lax.axis_index("dp")
        t = lax.axis_index("tp")
        self.y, self.z = d // NZ, lax.rem(d, NZ)
        self.h, self.x, self.c = t // (2 * NX), lax.rem(t // 2, NX), lax.rem(t, 2)
        self.d, self.t = d, t
        self.slot = self.h * NX + self.x

    def at(self, y=None, z=None, h=None, x=None, c=None):
        y = self.y if y is None else y
        z = self.z if z is None else z
        h = self.h if h is None else h
        x = self.x if x is None else x
        c = self.c if c is None else c
        return (y * NZ + z, h * (2 * NX) + x * 2 + c)

    def sibling(self):
        return self.at(c=1 - self.c)

    def flip(self):
        return self.at(h=1 - self.h)


def plus(value, step, size):
    return lax.rem(value + step, size)


def kernel(
    tb_in,
    slot_in,
    patches,
    conv,
    proj,
    out_ref,
    tb_ref,
    slot_ref,
    tokens,
    halves,
    pair_rows,
    grid_img,
    rests,
    weights,
    z_ref,
    fs_ref,
    pooled,
    proj_all,
    proj_cols,
    proj_perm,
    own_pool,
    by_image,
    rounded,
    result,
    half_ok,
    flip_ok,
    loc,
    ce_s,
    w_s,
    img_s,
    rest_s,
    proj_s,
    proj_cs,
    q_s,
    pool_s,
    pool_cs,
    ce_r,
    wz_r,
    wy_r,
    wd_r,
    gz_r,
    gx_r,
    rz_r,
    rx_r,
    pz_r,
    px_r,
    pd_r,
    qz_r,
    qy_r,
    oz_r,
    ox_r,
    oc_r,
    od_r,
):
    me = Place()
    c, h, x, y, z, d = me.c, me.h, me.x, me.y, me.z, me.d
    other = 1 - c
    sibling, flip = me.sibling(), me.flip()
    my_slot = me.slot
    flip_slot = (1 - h) * NX + x

    def remote(src, dst, send, recv, where):
        return pltpu.make_async_remote_copy(
            src_ref=src, dst_ref=dst, send_sem=send, recv_sem=recv, device_id=where, device_id_type=MESH
        )

    def await_recv(dst, recv):
        remote(dst, dst, recv, recv, sibling).wait_recv()

    def await_send(src, send):
        remote(src, src, send, send, sibling).wait_send()

    bits = (lax.rem(z, 2), lax.rem(z // 2, 2), z // 4)

    def across(m):
        return sum((1 - bit if m >> i & 1 else bit) * (1 << i) for i, bit in enumerate(bits))

    barrier = pltpu.get_barrier_semaphore()

    def greet(where):
        pl.semaphore_signal(barrier, inc=1, device_id=where, device_id_type=MESH)

    for k in range(1, NZ):
        greet(me.at(z=plus(z, k, NZ), c=1))
    for k in range(1, NX):
        greet(me.at(x=plus(x, k, NX), c=1))
    for k in range(1, NY):
        greet(me.at(y=plus(y, k, NY), c=1))

    @pl.when(c == 0)
    def _():
        greet(sibling)

    greet(me.at(h=1 - h, c=0))

    local = [
        pltpu.make_async_copy(patches, tokens.at[c], loc.at[0]),
        pltpu.make_async_copy(conv, halves.at[c], loc.at[1]),
        pltpu.make_async_copy(proj, proj_all.at[c, my_slot], loc.at[2]),
        pltpu.make_async_copy(tb_in, tb_ref, loc.at[3]),
        pltpu.make_async_copy(slot_in, slot_ref, loc.at[4]),
    ]
    for copy in local:
        copy.start()

    for copy in local:
        copy.wait()
    @pl.when(c == 1)
    def _():
        pl.semaphore_wait(barrier, 2 * (NZ - 1 + NX - 1 + NY - 1) + 1)
        pl.semaphore_signal(half_ok, inc=1, device_id=sibling, device_id_type=MESH)

    @pl.when(c == 0)
    def _():
        pl.semaphore_wait(half_ok, 1)

    def meet_other_half():
        @pl.when(c == 0)
        def _():
            pl.semaphore_wait(barrier, 2)
            pl.semaphore_signal(flip_ok, inc=1, device_id=sibling, device_id_type=MESH)

        @pl.when(c == 1)
        def _():
            pl.semaphore_wait(flip_ok, 1)


    ce_conv = remote(halves.at[c], halves.at[c], ce_s.at[0], ce_r.at[0], sibling)
    ce_conv.start()
    ce_img = remote(tokens.at[c], tokens.at[c], ce_s.at[1], ce_r.at[1], sibling)
    ce_img.start()
    own_proj = proj_all.at[c, my_slot]
    flip_proj = proj_all.at[c, flip_slot]

    def to_x(piece, send, recv):
        for k in range(1, NX):
            remote(piece, piece, send, recv, me.at(x=plus(x, k, NX))).start()

    def shard(dp, core):
        return weights.at[pl.ds(pl.multiple_of(dp * 288 + core * 144, 16), 144)]

    def w_piece(m, j=0):
        return shard(plus(y, NY - j, NY) * NZ + across(m), c)

    def q_piece(m, j=0):
        return proj_cols.at[plus(y, NY - j, NY) * NZ + across(m)]

    def to_z(piece, m, send, recvs, partners):
        for p in partners:
            remote(piece(m), piece(m), send, recvs.at[(m ^ p) - 1], me.at(z=across(p))).start()

    def w_to_sibling(m, j):
        remote(w_piece(m, j), w_piece(m, j), w_s, wd_r, sibling).start()

    def w_step(m, partners):
        if m:
            await_recv(w_piece(m), wz_r.at[m - 1])
        to_z(w_piece, m, w_s, wz_r, partners)
        for j in range(1, NY):
            remote(w_piece(m), w_piece(m), w_s, wy_r.at[2 * (j - 1) + m % 2], me.at(y=plus(y, j, NY))).start()
        w_to_sibling(m, 0)

    def w_rest(j, odd):
        await_recv(weights.at[pl.ds(0, 4 * 144)], wy_r.at[2 * (j - 1) + odd])
        for m in range(odd, NZ, 2):
            w_to_sibling(m, j)

    def q_step(m, partners):
        if m:
            await_recv(q_piece(m), qz_r.at[m - 1])
        to_z(q_piece, m, q_s, qz_r, partners)
        for j in range(1, NY):
            remote(q_piece(m), q_piece(m), q_s, qy_r, me.at(y=plus(y, j, NY))).start()

    def proj_along_x():
        await_recv(flip_proj, pz_r)
        to_x(flip_proj, proj_s, px_r)

    def proj_to_sibling():
        await_recv(proj_all.at[c, pl.ds(0, 2 * (NX - 1))], px_r)
        remote(proj_all.at[c], proj_all.at[c], proj_cs, pd_r, sibling).start()

    def proj_select():
        await_recv(proj_all.at[other], pd_r)
        holder = jnp.int32(0)
        for t in range(4 * NX):
            holder = jnp.where(tb_ref[t] == me.t, t, holder)
        q_piece(0)[...] = proj_all[lax.rem(holder, 2), holder // 2]

    await_recv(halves.at[other], ce_r.at[0])
    own_shard = w_piece(0)
    both = jnp.concatenate([halves[0], halves[1]], axis=0).astype(jnp.float32)
    both = jnp.concatenate([both, jnp.zeros((128, 96), jnp.float32)], axis=1)
    pair_rows[...] = both.T[:288].astype(jnp.bfloat16)
    own_shard[...] = pair_rows[pl.ds(pl.multiple_of(c * 144, 16), 144), :]
    w_step(0, (4, 2, 1))
    to_x(own_proj, proj_s, px_r)

    @pl.when(h == 1)
    def _():
        meet_other_half()
        remote(own_proj, own_proj, proj_s, pz_r, flip).start()


    await_recv(tokens.at[other], ce_r.at[1])
    mine = [
        jnp.where(c == 0, both[:, 0, :], both[:, 1, :]) for both in (tokens[i].astype(jnp.float32) for i in range(2))
    ]
    chip_tokens = jnp.concatenate(mine + [jnp.zeros((SLOT_ROWS - CHIP_ROWS, 1024), jnp.float32)], axis=0)

    def image(slot, first=0, count=SLOT_ROWS):
        return grid_img.at[pl.ds(pl.multiple_of(slot * SLOT_ROWS + first, 16), count)]

    image(my_slot, 0, BODY_ROWS)[...] = chip_tokens[:BODY_ROWS].astype(jnp.bfloat16)
    own_rest = chip_tokens[BODY_ROWS:CHIP_ROWS]
    rests[my_slot] = jnp.concatenate([own_rest[:, :512], own_rest[:, 512:]], axis=0).astype(jnp.bfloat16)
    to_x(image(my_slot, 0, BODY_ROWS), img_s, gx_r.at[0])
    to_x(rests.at[my_slot], rest_s, rx_r.at[0])

    def flip_cut(i):
        piece = image(my_slot, *CUTS[i])
        remote(piece, piece, img_s, gz_r.at[i], flip).start()

    def flip_rest():
        remote(rests.at[my_slot], rests.at[my_slot], rest_s, rz_r, flip).start()

    def image_step(i):
        piece = image(flip_slot, *CUTS[i])
        await_recv(piece, gz_r.at[i])
        to_x(piece, img_s, gx_r.at[1])

    def rest_step():
        await_recv(rests.at[flip_slot], rz_r)
        to_x(rests.at[flip_slot], rest_s, rx_r.at[1])

    def image_wait(which):
        await_recv(grid_img.at[pl.ds(0, (NX - 1) * BODY_ROWS)], gx_r.at[which])
        await_recv(rests.at[pl.ds(0, NX - 1)], rx_r.at[which])

    def put_rests(half):
        for i in range(NX):
            rest = rests[half * NX + i].astype(jnp.float32)
            rest = jnp.concatenate([rest[:8], rest[8:]], axis=1)
            rest = jnp.concatenate([rest, jnp.zeros((8, 1024), jnp.float32)], axis=0)
            image(half * NX + i, BODY_ROWS, 16)[...] = rest.astype(jnp.bfloat16)

    def multiply(half):
        put_rests(half)
        rows = pl.ds(pl.multiple_of(half * (NX * SLOT_ROWS), 64), NX * SLOT_ROWS)

        @pl.loop(0, 5)
        def _(n):
            rhs = jnp.concatenate(
                [
                    weights[pl.ds(pl.multiple_of(n * 2048, 1024), 1024), :],
                    weights[pl.ds(pl.multiple_of(n * 2048 + 1024, 1024), 1024), :],
                ],
                axis=1,
            )
            prod = jnp.dot(grid_img[rows, :], rhs, preferred_element_type=jnp.float32)
            z_ref[2 * n, rows, :] = prod[:, :128]
            z_ref[2 * n + 1, rows, :] = prod[:, 128:]

    @pl.when(h == 0)
    def _():
        meet_other_half()
        remote(own_proj, own_proj, proj_s, pz_r, flip).start()

    row = lax.broadcasted_iota(jnp.int32, (1024, 128), 0)
    lane = lax.broadcasted_iota(jnp.int32, (1024, 128), 1)
    first = tb_ref[2 * my_slot] * 64
    second = tb_ref[2 * my_slot + 1] * 64 - 64
    wanted = lane + jnp.where(lane < 64, first, second)
    weights[pl.ds(9 * 1024, 1024), :] = jnp.where(row == wanted, 1.0, 0.0).astype(jnp.bfloat16)
    w_step(4, (2, 1))
    @pl.when(h == 1)
    def _():
        flip_cut(0)

    @pl.when(h == 0)
    def _():
        flip_cut(0)
        flip_cut(1)
        flip_rest()

    w_step(2, (1,))
    w_step(6, (1,))
    @pl.when(h == 1)
    def _():
        flip_cut(1)
        flip_rest()

    proj_along_x()
    w_step(1, ())
    w_step(5, ())
    proj_to_sibling()
    @pl.when(h == 0)
    def _():
        proj_select()
        q_step(0, (4, 1, 2, 3))

    @pl.when(h == 1)
    def _():
        image_step(0)

    w_step(3, ())
    w_step(7, ())
    @pl.when(h == 1)
    def _():
        proj_select()
        q_step(0, (4, 2, 1))


    @pl.when(h == 0)
    def _():
        image_step(0)

    for j in range(1, NY):
        w_rest(j, 0)
    image_step(1)
    rest_step()
    @pl.when(h == 0)
    def _():
        q_step(4, (1, 2, 3))

    @pl.when(h == 0)
    def _():
        for m in (1, 2, 3):
            q_step(m, ())

    for j in range(1, NY):
        w_rest(j, 1)
    await_recv(weights.at[pl.ds(0, NY * NZ * 144)], wd_r)
    image_wait(0)
    multiply(h)
    image_wait(1)
    @pl.when(h == 0)
    def _():
        for m in (5, 6, 7):
            q_step(m, ())

    multiply(1 - h)

    column = lax.broadcasted_iota(jnp.int32, (GRID, 128), 0)

    def product(tap, gy):
        return z_ref[tap, pl.ds((gy // 3) * SLOT_ROWS + (gy % 3) * GRID, GRID), :]

    for gy in range(0, GRID, 2):
        total = jnp.zeros((GRID, 128), jnp.float32)
        for row_y in (gy, gy + 1):
            parts = []
            for kx in range(3):
                part = None
                for ky in range(3):
                    if 0 <= row_y + ky - 1 < GRID:
                        value = product(3 * ky + kx, row_y + ky - 1)
                        part = value if part is None else part + value
                parts.append(part)
            left = jnp.where(column == 0, 0.0, pltpu.roll(parts[0], 1, 0))
            right = jnp.where(column == GRID - 1, 0.0, pltpu.roll(parts[2], GRID - 1, 0))
            value = parts[1] + left + right
            total = total + product(9, row_y) + value / (1.0 + jnp.exp(-value))
        fs_ref[pl.ds((gy // 2) * GRID, GRID), :] = total
    mean = (fs_ref[pl.ds(0, 144, stride=2), :] + fs_ref[pl.ds(1, 144, stride=2), :]) * 0.25
    own_pool[...] = mean.astype(jnp.bfloat16)

    def pool_to_x(piece, dst, half):
        for k in range(1, NX):
            remote(piece, dst, pool_s, ox_r.at[half], me.at(x=plus(x, k, NX), c=1)).start()

    remote(own_pool, pooled.at[c, my_slot], pool_s, oz_r.at[c], me.at(h=1 - h, c=1)).start()
    pool_to_x(own_pool, pooled.at[c, my_slot], 0)

    @pl.when(c == 0)
    def _():
        remote(own_pool, pooled.at[0, my_slot], pool_cs, oc_r, sibling).start()

    @pl.when(c == 1)
    def _():
        pooled[1, my_slot] = own_pool[...]

    @pl.when(h == 1)
    def _():
        q_step(4, (2, 1))

    @pl.when(h == 1)
    def _():
        q_step(2, (1,))
        q_step(6, (1,))

    @pl.when(h == 1)
    def _():
        for m in (1, 5, 3, 7):
            q_step(m, ())

    @pl.when(c == 1)
    def _():
        for i in (1, 0):
            flip_pool = pooled.at[i, flip_slot]
            await_recv(flip_pool, oz_r.at[i])
            pool_to_x(flip_pool, flip_pool, 1)

    def pool_of_half(half):
        return pooled.at[:, pl.ds((h if half == 0 else 1 - h) * NX, NX)]

    def pool_to_first(half):
        await_recv(pooled.at[:, pl.ds(0, NX - 1)], ox_r.at[half])
        remote(pool_of_half(half), pool_of_half(half), pool_cs, od_r.at[half], sibling).start()

    @pl.when(c == 1)
    def _():
        await_recv(pooled.at[0, my_slot], oc_r)
        pool_to_first(0)

    await_recv(proj_cols.at[pl.ds(0, (NY - 1) * NZ)], qy_r)

    for t in range(4 * NX):
        block = tb_ref[t]
        proj_perm[pl.ds(t * 64, 32), :] = proj_cols[2 * block]
        proj_perm[pl.ds(t * 64 + 32, 32), :] = proj_cols[2 * block + 1]

    @pl.when(c == 0)
    def _():
        await_recv(pool_of_half(0), od_r.at[0])

    def project(half):
        first = (h if half == 0 else 1 - h) * NX
        rows = pl.ds(pl.multiple_of(first * 128, 512), 512)
        lhs = jnp.concatenate(
            [jnp.concatenate([pooled[i, first + s] for s in range(NX)], axis=1) for i in range(2)], axis=0
        )
        return jnp.dot(lhs, proj_perm[rows, :], preferred_element_type=jnp.float32)

    half_sum = project(0)
    for i in range(2):
        by_image[i] = half_sum[144 * i : 144 * (i + 1)]
    @pl.when(c == 1)
    def _():
        pool_to_first(1)

    @pl.when(c == 0)
    def _():
        await_recv(pool_of_half(1), od_r.at[1])

    half_sum = project(1)
    for i in range(2):
        rounded[i] = (by_image[i] + half_sum[144 * i : 144 * (i + 1)]).astype(jnp.bfloat16)
    results = []
    for slot in range(2):
        result[slot] = rounded[slot_ref[slot]]
        results.append(pltpu.make_async_copy(result.at[slot], out_ref.at[slot], loc.at[slot]))
        results[-1].start()

    ce_conv.wait_send()
    ce_img.wait_send()
    await_send(weights.at[pl.ds(0, (NZ - 1 + (NY - 1) * NZ + NY * NZ) * 144)], w_s)
    await_send(grid_img.at[pl.ds(0, (2 * (NX - 1) + 1) * BODY_ROWS)], img_s)
    await_send(rests.at[pl.ds(0, 2 * (NX - 1) + 1)], rest_s)
    await_send(proj_all.at[c, pl.ds(0, 2 * (NX - 1) + 1)], proj_s)
    await_send(proj_all.at[c], proj_cs)
    await_send(proj_cols.at[pl.ds(0, NZ - 1 + (NY - 1) * NZ)], q_s)
    @pl.when(c == 0)
    def _():
        await_send(pooled.at[0, pl.ds(0, NX)], pool_s)
        await_send(own_pool, pool_cs)

    @pl.when(c == 1)
    def _():
        await_send(pooled.at[:, pl.ds(0, (3 * (NX - 1) + 1) // 2)], pool_s)
        await_send(pooled, pool_cs)

    for copy in results:
        copy.wait()


def per_device(patches, image_slot, trainer_blocks, conv_weight, proj_weight):
    dma = pltpu.SemaphoreType.DMA
    anywhere = pl.BlockSpec(memory_space=pl.ANY)
    bf16, f32 = jnp.bfloat16, jnp.float32
    sems = [
        dma((2,)),
        dma,
        dma,
        dma,
        dma,
        dma,
        dma,
        dma,
        dma,
        dma((2,)),
        dma((NZ - 1,)),
        dma((2 * (NY - 1),)),
        dma,
        dma((len(CUTS),)),
        dma((2,)),
        dma,
        dma((2,)),
        dma,
        dma,
        dma,
        dma((NZ - 1,)),
        dma,
        dma((2,)),
        dma((2,)),
        dma,
        dma((2,)),
    ]
    return pl.pallas_call(
        kernel,
        out_shape=jax.ShapeDtypeStruct((2, 144, 512), bf16),
        in_specs=[pl.BlockSpec(memory_space=pltpu.HBM)] * 5,
        out_specs=anywhere,
        scratch_shapes=[
            pltpu.SMEM((16,), jnp.int32),
            pltpu.SMEM((2,), jnp.int32),
            pltpu.VMEM((2, 36, 2, 1024), bf16),
            pltpu.VMEM((2, 64, 288), bf16),
            pltpu.VMEM((288, 128), bf16),
            pltpu.VMEM((SLOTS * SLOT_ROWS, 1024), bf16),
            pltpu.VMEM((SLOTS, 16, 512), bf16),
            pltpu.VMEM((10 * 1024, 128), bf16),
            pltpu.VMEM((10, SLOTS * SLOT_ROWS, 128), f32),
            pltpu.VMEM((296, 128), f32),
            pltpu.VMEM((2, SLOTS, 144, 128), bf16),
            pltpu.VMEM((2, SLOTS, 32, 512), bf16),
            pltpu.VMEM((NY * NZ, 32, 512), bf16),
            pltpu.VMEM((1024, 512), bf16),
            pltpu.VMEM((144, 128), bf16),
            pltpu.VMEM((2, 144, 512), f32),
            pltpu.VMEM((2, 144, 512), bf16),
            pltpu.VMEM((2, 144, 512), bf16),
            pltpu.SemaphoreType.REGULAR,
            pltpu.SemaphoreType.REGULAR,
            dma((5,)),
        ]
        + sems,
        compiler_params=pltpu.CompilerParams(
            collective_id=0, has_side_effects=True, vmem_limit_bytes=40 * 1024 * 1024
        ),
        cost_estimate=pl.CostEstimate(flops=2_000_000_000, bytes_accessed=600_000, transcendentals=73728),
        name="vision",
    )(*(pltpu.with_memory_space_constraint(a, pltpu.HBM) for a in (trainer_blocks, image_slot, jnp.transpose(patches, (1, 0, 2)), conv_weight.T, proj_weight)))


def solution(mesh):
    placed = (P("dp", "tp", None), P("dp"), P(), P("dp", "tp"), P("dp", "tp"))
    return jax.shard_map(
        per_device, mesh=mesh, in_specs=placed, out_specs=P("dp", None, "tp"), check_vma=False
    )
```
